32 devices in a mesh: groups: 2 (over y), wide: 4 (over z), narrow: 4 (over x, core).
Axes of the slice: x: 2, y: 2, z: 4, core: 2. Of those that a mesh axis runs over, the one named last changes fastest.
Arguments:
- tokens: bfloat16 [8192, 8192], P(('groups', 'wide'), 'narrow'), parts along dimension 0, may hold values from -6 to 6
- value_weight: bfloat16 [8192, 1024], P('narrow'), may hold values from -0.0625 to 0.0625
- adapter_down_factors: bfloat16 [16, 8192, 64], P(('groups', 'wide'), 'narrow'), parts along dimension 0, may hold values from -0.0625 to 0.0625
- adapter_up_factors: bfloat16 [16, 64, 1024], P(('groups', 'wide'), None, 'narrow'), parts along dimension 0, may hold values from -0.75 to 0.75
- adapter_choice_index: int32 [256], P('groups'), parts along dimension 0, may hold values from 0 to 7
- adapter_mask: int32 [256], P('groups'), parts along dimension 0, may hold values 0 or 1
- prompt_token_length: int32 [256], P('groups'), parts along dimension 0, may hold values from 1 to 32, 2560 in all
Outputs:
- values: bfloat16 [8192, 1024], P(('groups', 'wide'), 'narrow'), parts along dimension 0
The draws below stay inside these ranges and needn't reach their ends.
There are 2 independent parts, one for each index of `groups`. The reference program is written for one: setup_inputs(seed, part) draws one part's arguments, and reference() takes and returns one part's arrays. A program takes and returns all parts, laid end to end along the dimension named above; an argument that names none is the same for every part. Nothing has to cross between parts.
All inputs are finite; a program needn't handle non-finite values.
Results may differ from the reference program's by a relative error of at most 0.001.
Values may be sent and summed in bfloat16 or wider, within the bound.
No kernel may reach another device: no remote copies, remote signals or barrier semaphores. Data moves between devices by JAX's collectives and lax.ppermute only.
A program may use at most 64 MiB of HBM per device.

```python
import math
import jax
import jax.numpy as jnp
import numpy as np
from jax import lax

MODEL_WIDTH = 8192
ADAPTER_RANK = 64
ADP_DEV = 2
P_DEV = 32
LEN = 32
VALUE_WIDTH = 1024
ADAPTER_COUNT = 8
PROMPT_COUNT = 128
TOKENS = 4096
N_WIDE = 4


def with_ends(result, own_key, smallest, largest):
    longest = result.shape.index(max(result.shape))
    spots = []
    for shift in (0, 1):
        where = [jax.random.randint(jax.random.fold_in(own_key, axis), (), 0, length) for axis, length in enumerate(result.shape)]
        where[longest] = (where[longest] + shift) % result.shape[longest]
        spots.append(tuple(where))
    return result.at[spots[0]].set(smallest).at[spots[1]].set(largest)


def levels(stream_key, extent, shards, smallest, top_value):
    loudness = 1.0
    for axis_at, parts in shards:
        steps = jax.random.uniform(jax.random.fold_in(jax.random.fold_in(stream_key, 6), axis_at), (parts,), jnp.float32, smallest / len(shards), top_value / len(shards))
        loudness = loudness * jnp.repeat(jnp.exp(steps), extent[axis_at] // parts).reshape((-1,) + (1,) * (len(extent) - 1 - axis_at))
    return loudness


def rank_table(amount, slope):
    portions = [(1 << 20) // math.isqrt(grade ** slope) + 1 for grade in range(1, amount + 1)]
    deviation = 1 + sum(portions) // (1 << 30)
    return np.cumsum(np.array([max(1, weight // deviation) for weight in portions]))


def skewed_ids(own_key, dims, count, slope):
    table = rank_table(count, slope)
    ticket = jax.random.randint(jax.random.fold_in(own_key, 1), dims, 0, int(table[count - 1]))
    grade = jnp.searchsorted(jnp.asarray(table, jnp.int32), ticket, side="right")
    return jax.random.permutation(jax.random.fold_in(own_key, 2), count)[grade].astype(jnp.int32)


def length_profile(count, total, bound, skew):
    weights = [(1 << 20) // math.isqrt(standing ** skew) + 1 for standing in range(2, count + 1)]
    rest, counts = total - bound - (count - 1), [1] * (count - 1)
    while rest > 0:
        candidates = [i for i in range(count - 1) if counts[i] < bound]
        whole, left = sum([weights[i] for i in candidates]), rest
        for i in candidates:
            addition = min(bound - counts[i], max(1, left * weights[i] // whole), rest)
            counts[i] = counts[i] + addition
            rest = rest - addition
    return np.array([bound] + counts)


def uneven(stream_key, amount, total, most, skew):
    if amount == 2:
        one = jax.random.randint(stream_key, (), max(1, total - most), min(most, total - 1) + 1)
        return jnp.stack([one, total - one])
    sizes = jnp.asarray(length_profile(amount, total, most, skew), jnp.int32)
    twos = (amount - 1) // 2
    giver, receiver = sizes[1:1 + 2 * twos:2], sizes[2:2 + 2 * twos:2]
    margin = jnp.minimum(giver - 1, most - receiver)
    shifted = jax.random.randint(jax.random.fold_in(stream_key, 1), (twos,), 0, 1 << 20) % (margin + 1)
    sizes = sizes.at[1:1 + 2 * twos:2].set(giver - shifted).at[2:2 + 2 * twos:2].set(receiver + shifted)
    return sizes[jax.random.permutation(jax.random.fold_in(stream_key, 2), amount)]


def gaussian(own_key, extent, width, bound, cuts=(), kind=jnp.bfloat16):
    result = width * jax.random.normal(own_key, extent, jnp.float32)
    if cuts:
        result = result * levels(own_key, extent, cuts, -0.22, 0.18)
    return jnp.clip(result, -bound, bound).astype(kind)


def setup_inputs(seed: int = 0, part: int = 0) -> dict:
    keys = jax.random.split(jax.random.key(seed), 8)
    part_keys = jax.random.split(jax.random.fold_in(keys[7], part), 8)
    tokens = gaussian(part_keys[0], (TOKENS, MODEL_WIDTH), 1.0, 6.0, ((0, 4), (1, 4)))
    value_weight = gaussian(keys[1], (MODEL_WIDTH, VALUE_WIDTH), MODEL_WIDTH ** -0.5, 0.0625, ((0, 4),))
    adapter_down_factors = gaussian(part_keys[2], (ADAPTER_COUNT, MODEL_WIDTH, ADAPTER_RANK), MODEL_WIDTH ** -0.5, 0.0625, ((0, 4), (1, 4)))
    adapter_up_factors = gaussian(part_keys[3], (ADAPTER_COUNT, ADAPTER_RANK, VALUE_WIDTH), ADAPTER_RANK ** -0.5, 0.75, ((0, 4), (2, 4)))
    adapter_choice_index = with_ends(skewed_ids(part_keys[4], (PROMPT_COUNT,), ADAPTER_COUNT, 1), jax.random.fold_in(part_keys[4], 3), 0, ADAPTER_COUNT - 1).astype(jnp.int32)
    adapter_mask = with_ends((jax.random.randint(part_keys[5], (PROMPT_COUNT,), 0, 4) < 3).astype(jnp.int32), jax.random.fold_in(part_keys[5], 1), 0, 1)
    prompt_token_length = uneven(part_keys[6], PROMPT_COUNT, PROMPT_COUNT * LEN * 5 // 8, LEN, 2).astype(jnp.int32)
    return dict(tokens=tokens, value_weight=value_weight, adapter_down_factors=adapter_down_factors, adapter_up_factors=adapter_up_factors, adapter_choice_index=adapter_choice_index, adapter_mask=adapter_mask, prompt_token_length=prompt_token_length)


def request_table(adapter_choice_index, adapter_mask, wide_count, per_device, owner_portion):
    requests = adapter_choice_index.reshape(wide_count, per_device).astype(jnp.int32)
    wanted = adapter_mask.reshape(wide_count, per_device) == 1
    owners = requests // owner_portion
    owner_range = jnp.arange(wide_count, dtype=jnp.int32)
    matches = wanted[:, None, :] & (owners[:, None, :] == owner_range[None, :, None])
    earliest = jnp.argmax(matches.astype(jnp.int32), axis=2).astype(jnp.int32)
    prompt_range = jnp.arange(per_device, dtype=jnp.int32)
    chosen = jnp.sum(jnp.where(prompt_range[None, None, :] == earliest[:, :, None], requests[:, None, :], 0), axis=2).astype(jnp.int32)
    granted = jnp.where(jnp.any(matches, axis=2), chosen, -1).astype(jnp.int32)
    applied_delta = jnp.any(matches & (requests[:, None, :] == granted[:, :, None]), axis=1)
    return granted, applied_delta


def reference(tokens, value_weight, adapter_down_factors, adapter_up_factors, adapter_choice_index, adapter_mask, prompt_token_length):
    granted, applied_delta = request_table(adapter_choice_index, adapter_mask, N_WIDE, P_DEV, ADP_DEV)
    base_sums = jnp.dot(tokens, value_weight, preferred_element_type=jnp.float32)
    prompt_blocks = tokens.reshape(PROMPT_COUNT, LEN, MODEL_WIDTH)

    def one_prompt(prompt_item):
        prompt_rows, adapter_item = prompt_item
        down_factor_block = lax.dynamic_index_in_dim(adapter_down_factors, adapter_item, 0, keepdims=False)
        up_factor_block = lax.dynamic_index_in_dim(adapter_up_factors, adapter_item, 0, keepdims=False)
        shrunk = jnp.dot(prompt_rows, down_factor_block, preferred_element_type=jnp.float32)
        return jnp.dot(shrunk, up_factor_block.astype(jnp.float32), precision=lax.Precision.HIGHEST)

    delta_outputs = lax.map(one_prompt, (prompt_blocks, adapter_choice_index.astype(jnp.int32)))
    adapter_gate = applied_delta.reshape(PROMPT_COUNT).astype(jnp.float32)
    delta_outputs = delta_outputs * adapter_gate[:, None, None]
    inside = jnp.arange(LEN, dtype=jnp.int32)[None, :] < prompt_token_length.astype(jnp.int32)[:, None]
    summed = base_sums.reshape(PROMPT_COUNT, LEN, VALUE_WIDTH) + delta_outputs
    values = jnp.where(inside[:, :, None], summed, jnp.float32(0.0))
    return values.reshape(TOKENS, VALUE_WIDTH).astype(jnp.bfloat16)
```

```python
import functools

import jax
import jax.numpy as jnp
from jax import lax
from jax.experimental import pallas as pl
from jax.experimental.pallas import tpu as pltpu
from jax.sharding import PartitionSpec as P

LEN = 32
CHUNKS = 2
VMEM = pltpu.VMEM
F32 = jnp.float32
BF16 = jnp.bfloat16


def whole_block(array_memory=VMEM):
    return pl.BlockSpec(memory_space=array_memory)


def pack_kernel(wide_count, per_device, place_ref, choice_ref, mask_ref, down_ref, up_ref, *messages):
    owner_portion, rank, features = down_ref.shape
    rows = rank // CHUNKS
    me = place_ref[0]
    choice = choice_ref[...]
    prompt = lax.broadcasted_iota(jnp.int32, choice.shape, 1)
    local = choice - me * owner_portion
    wanted = (mask_ref[...] == 1) & (local >= 0) & (local < owner_portion)
    top = jnp.float32(2.0**24)
    key = jnp.where(wanted, (prompt * owner_portion + local).astype(F32), top)
    for shift in range(wide_count):
        reader = lax.rem(me + shift, wide_count)
        low = reader * per_device
        inside = (prompt >= low) & (prompt < low + per_device)
        first = jnp.min(jnp.where(inside, key, top))
        found = jnp.where(first < top, first, 0.0).astype(jnp.int32)
        adapter = lax.rem(found, owner_portion)
        for chunk in range(CHUNKS):
            out = messages[shift * CHUNKS + chunk]
            out[:, :features] = down_ref[adapter, pl.ds(chunk * rows, rows), :]
            out[:, features:] = up_ref[adapter, pl.ds(chunk * rows, rows), :]


def pack_messages(place, choice, mask, down, up, wide_count, per_device):
    rank, features = down.shape[1:]
    columns = up.shape[2]
    message = jax.ShapeDtypeStruct((rank // CHUNKS, features + columns), BF16)
    count = wide_count * CHUNKS
    out = pl.pallas_call(
        functools.partial(pack_kernel, wide_count, per_device),
        out_shape=[message] * count,
        in_specs=[whole_block(pltpu.SMEM)] + [whole_block()] * 4,
        out_specs=[whole_block()] * count,
        compiler_params=pltpu.CompilerParams(vmem_limit_bytes=24 * 2**20),
        cost_estimate=pl.CostEstimate(flops=0, bytes_accessed=2 * 2**20, transcendentals=0),
        name="pack_messages",
    )(place, choice, mask, down, up)
    return [out[shift * CHUNKS : (shift + 1) * CHUNKS] for shift in range(wide_count)]


def pair_kernel(order_ref, tokens_ref, first_ref, second_ref, send_ref, keep_ref):
    rows = tokens_ref[...]
    send_ref[...] = jnp.dot(rows, first_ref[...], preferred_element_type=F32)
    keep_ref[...] = jnp.dot(rows, second_ref[...], preferred_element_type=F32)


def matmul_pair(tokens, weight, order, columns, name):
    row_total, features = tokens.shape
    block = 256
    out = jax.ShapeDtypeStruct((row_total, columns), F32)
    out_spec = pl.BlockSpec((block, columns), lambda r, order: (r, 0))
    return pl.pallas_call(
        pair_kernel,
        out_shape=[out, out],
        grid_spec=pltpu.PrefetchScalarGridSpec(
            num_scalar_prefetch=1,
            grid=(row_total // block,),
            in_specs=[
                pl.BlockSpec((block, features), lambda r, order: (r, 0)),
                pl.BlockSpec((features, columns), lambda r, order: (0, order[0])),
                pl.BlockSpec((features, columns), lambda r, order: (0, order[1])),
            ],
            out_specs=[out_spec, out_spec],
        ),
        compiler_params=pltpu.CompilerParams(vmem_limit_bytes=24 * 2**20),
        cost_estimate=pl.CostEstimate(
            flops=4 * row_total * features * columns,
            bytes_accessed=row_total * features * 2 + features * columns * 4 + row_total * columns * 8,
            transcendentals=0,
        ),
        name=name,
    )(order, tokens, weight, weight)


def shrink_kernel(tokens_ref, chosen_ref, *refs):
    messages, out_ref, stacked = refs[:-2], refs[-2], refs[-1]
    rows = out_ref.shape[0]
    features = tokens_ref.shape[1]

    @pl.when(pl.program_id(0) == 0)
    def _():
        for at, message in enumerate(messages):
            stacked[pl.ds(at * rows, rows), :] = message[:, :features]

    sums = lax.dot_general(
        stacked[...], tokens_ref[...], (((1,), (1,)), ((), ())), preferred_element_type=F32
    )
    total = None
    for at in range(len(messages)):
        term = jnp.where(chosen_ref[pl.ds(at, 1), :] > 0, sums[at * rows : (at + 1) * rows, :], 0.0)
        total = term if total is None else total + term
    out_ref[...] = total


def shrink(tokens, chosen, messages, columns):
    row_total, features = tokens.shape
    count = len(messages)
    rows = messages[0].shape[0]
    block = 256
    return pl.pallas_call(
        shrink_kernel,
        out_shape=jax.ShapeDtypeStruct((rows, row_total), F32),
        grid=(row_total // block,),
        in_specs=[
            pl.BlockSpec((block, features), lambda r: (r, 0)),
            pl.BlockSpec((count, block), lambda r: (0, r)),
        ]
        + [pl.BlockSpec((rows, features + columns), lambda r: (0, 0))] * count,
        out_specs=pl.BlockSpec((rows, block), lambda r: (0, r)),
        scratch_shapes=[VMEM((count * rows, features), BF16)],
        compiler_params=pltpu.CompilerParams(vmem_limit_bytes=32 * 2**20),
        cost_estimate=pl.CostEstimate(
            flops=2 * row_total * features * count * rows,
            bytes_accessed=row_total * features * 2 + count * rows * (features + columns) * 2,
            transcendentals=0,
        ),
        name="shrink",
    )(tokens, chosen, *messages)


def finish_kernel(base_count, shrunk_counts, count, features, length_ref, chosen_ref, *refs):
    refs = list(refs)
    factors = refs[len(refs) - len(shrunk_counts) :]
    out_ref = refs[len(refs) - len(shrunk_counts) - 1]
    bases = [refs.pop(0) for _ in range(base_count)]
    total = bases[0][...]
    for base in bases[1:]:
        total = total + base[...]
    per_block = out_ref.shape[0] // LEN
    for terms, stacked in zip(shrunk_counts, factors):
        parts = [refs.pop(0) for _ in range(terms)]
        messages = [refs.pop(0) for _ in range(count)]
        rows = messages[0].shape[0]
        half = count * rows

        @pl.when(pl.program_id(0) == 0)
        def _(messages=messages, rows=rows, half=half, stacked=stacked):
            for at, message in enumerate(messages):
                factor = message[:, features:]
                stacked[pl.ds(at * rows, rows), :] = factor
                stacked[pl.ds(half + at * rows, rows), :] = factor

        shrunk = parts[0][...]
        for part in parts[1:]:
            shrunk = shrunk + part[...]
        spread = jnp.concatenate(
            [jnp.where(chosen_ref[pl.ds(at, 1), :] > 0, shrunk, 0.0) for at in range(count)], axis=0
        )
        high = spread.astype(BF16)
        low = (spread - high.astype(F32)).astype(BF16)
        both = jnp.concatenate([high, low], axis=0)
        total = total + lax.dot_general(
            both, stacked[...], (((0,), (0,)), ((), ())), preferred_element_type=F32
        )
    position = lax.broadcasted_iota(jnp.int32, (LEN, out_ref.shape[1]), 0)
    first = pl.program_id(0) * per_block
    for prompt in range(per_block):
        piece = total[prompt * LEN : (prompt + 1) * LEN, :]
        live = position < length_ref[first + prompt]
        out_ref[pl.ds(prompt * LEN, LEN), :] = jnp.where(live, piece, 0.0).astype(out_ref.dtype)


def finish(lengths, chosen, bases, shrunk, messages, features, out_dtype=BF16):
    row_total, columns = bases[0].shape
    count = len(messages[0])
    rows = messages[0][0].shape[0]
    block = 512
    wide_rows = pl.BlockSpec((block, columns), lambda r: (r, 0))
    in_specs = [whole_block(pltpu.SMEM), pl.BlockSpec((count, block), lambda r: (0, r))]
    in_specs += [wide_rows] * len(bases)
    operands = list(bases)
    for parts, sent in zip(shrunk, messages):
        in_specs += [pl.BlockSpec((rows, block), lambda r: (0, r))] * len(parts)
        in_specs += [pl.BlockSpec((rows, features + columns), lambda r: (0, 0))] * count
        operands += list(parts) + list(sent)
    return pl.pallas_call(
        functools.partial(finish_kernel, len(bases), [len(parts) for parts in shrunk], count, features),
        out_shape=jax.ShapeDtypeStruct((row_total, columns), out_dtype),
        grid=(row_total // block,),
        in_specs=in_specs,
        out_specs=wide_rows,
        scratch_shapes=[VMEM((2 * count * rows, columns), BF16)] * len(shrunk),
        compiler_params=pltpu.CompilerParams(vmem_limit_bytes=32 * 2**20),
        cost_estimate=pl.CostEstimate(
            flops=4 * row_total * columns * count * rows * len(shrunk),
            bytes_accessed=row_total * columns * 4 * (len(bases) + 1),
            transcendentals=0,
        ),
        name="finish",
    )(lengths, chosen, *operands)


def on_device(
    tokens,
    value_weight,
    adapter_down_factors,
    adapter_up_factors,
    adapter_choice_index,
    adapter_mask,
    prompt_token_length,
):
    wide_count = lax.axis_size("wide")
    narrow_count = lax.axis_size("narrow")
    wide_at = lax.axis_index("wide")
    narrow_at = lax.axis_index("narrow")
    owner_portion = adapter_down_factors.shape[0]
    row_total, features = tokens.shape
    per_device = row_total // LEN
    columns = adapter_up_factors.shape[2]

    place = jnp.full((1,), wide_at, jnp.int32)
    down = jnp.swapaxes(adapter_down_factors, 1, 2)
    sent = pack_messages(
        place,
        adapter_choice_index.reshape(1, -1),
        adapter_mask.reshape(1, -1),
        down,
        adapter_up_factors,
        wide_count,
        per_device,
    )
    held = [[sent[0][chunk]] for chunk in range(CHUNKS)]
    for chunk in range(CHUNKS):
        for shift in range(1, wide_count):
            ring = [(at, (at + shift) % wide_count) for at in range(wide_count)]
            held[chunk].append(lax.ppermute(sent[shift][chunk], "wide", ring))

    my_choice = lax.dynamic_slice_in_dim(adapter_choice_index, wide_at * per_device, per_device)
    my_mask = lax.dynamic_slice_in_dim(adapter_mask, wide_at * per_device, per_device)
    my_lengths = lax.dynamic_slice_in_dim(prompt_token_length, wide_at * per_device, per_device)
    owners = (wide_at - jnp.arange(wide_count, dtype=jnp.int32) + wide_count) % wide_count
    local = my_choice[None, :] - owners[:, None] * owner_portion
    matches = (my_mask[None, :] == 1) & (local >= 0) & (local < owner_portion)
    order = jnp.arange(per_device, dtype=jnp.int32)[None, :]
    first = jnp.min(
        jnp.where(matches, order * owner_portion + local, per_device * owner_portion), axis=1
    )
    granted = first % owner_portion
    chosen_prompt = (matches & (local == granted[:, None])).astype(F32)
    chosen = jnp.repeat(chosen_prompt, LEN, axis=1)

    if narrow_count == 4:
        core = [(at, at ^ 1) for at in range(4)]
        across = [(at, at ^ 2) for at in range(4)]
        other_chip, other_core = narrow_at ^ 2, narrow_at ^ 1
        far = jnp.stack([other_chip ^ 1, other_chip]).astype(jnp.int32)
        near = jnp.stack([other_core, narrow_at]).astype(jnp.int32)
        far_send, far_keep = matmul_pair(tokens, value_weight, far, columns, "far_columns")
        far_sum = far_keep + lax.ppermute(far_send, "narrow", core)
        crossed = lax.ppermute(far_sum, "narrow", across)
        near_send, near_keep = matmul_pair(tokens, value_weight, near, columns, "near_columns")
        bases = [near_keep, lax.ppermute(near_send, "narrow", core), crossed]
    else:
        partial_value = jnp.dot(tokens, value_weight, preferred_element_type=F32)
        bases = [lax.psum_scatter(partial_value, "narrow", scatter_dimension=1, tiled=True)]

    shrunk = []
    for chunk in range(CHUNKS):
        part = shrink(tokens, chosen, held[chunk], columns)
        if narrow_count == 4:
            part = part + lax.ppermute(part, "narrow", core)
            shrunk.append([part, lax.ppermute(part, "narrow", across)])
        else:
            shrunk.append([lax.psum(part, "narrow")])
    return finish(my_lengths, chosen, bases, shrunk, held, features)


def solution(mesh):
    placed = (
        P(("groups", "wide"), "narrow"),
        P("narrow", None),
        P(("groups", "wide"), "narrow", None),
        P(("groups", "wide"), None, "narrow"),
        P("groups"),
        P("groups"),
        P("groups"),
    )
    return jax.shard_map(
        on_device,
        mesh=mesh,
        in_specs=placed,
        out_specs=P(("groups", "wide"), "narrow"),
        check_vma=False,
    )
```

```python
import functools

import jax
import jax.numpy as jnp
from jax import lax
from jax.experimental import pallas as pl
from jax.experimental.pallas import tpu as pltpu
from jax.sharding import PartitionSpec as P

LEN = 32
CHUNKS = 1
LIMIT = 20 * 2**20
VMEM = pltpu.VMEM
F32 = jnp.float32
BF16 = jnp.bfloat16
STEPS = 32767.0
SMALL = pl.CostEstimate(flops=1, bytes_accessed=1, transcendentals=0)


def whole_block(array_memory=VMEM):
    return pl.BlockSpec(memory_space=array_memory)


def in_hbm(array):
    return pltpu.with_memory_space_constraint(array, pltpu.HBM)


def half_columns(weight_ref, chip, half):
    return weight_ref.at[:, pl.ds(pl.multiple_of(chip * half, half), half)]


def first_kernel(wide_count, per_device, paired, *refs):
    message_count = wide_count * CHUNKS
    loads_in, refs = refs[:4], refs[4:]
    if paired:
        tokens_hbm, weight_hbm, *refs = refs
    messages, refs = refs[:message_count], refs[message_count:]
    if paired:
        sums, refs = refs[:4], refs[4:]
    choice_ref, mask_ref, down_ref, up_ref, load_sem, message_sem = refs[:6]
    owner_portion, rank, features = down_ref.shape
    columns = up_ref.shape[2]
    rows = rank // CHUNKS
    loads = [
        pltpu.make_async_copy(source, target, load_sem.at[at])
        for at, (source, target) in enumerate(zip(loads_in, refs[:4]))
    ]
    for copy in loads:
        copy.start()
    if paired:
        tokens_ref, weight_ref, token_sem, weight_sem = refs[6:]
        narrow_at = lax.axis_index("narrow")
        mine = lax.rem(narrow_at, 2)
        chips = ((narrow_at // 2) ^ 1, narrow_at // 2)
        weight_copies = [
            pltpu.make_async_copy(
                half_columns(weight_hbm, chip, 2 * columns), weight_ref.at[half], weight_sem.at[half]
            )
            for half, chip in enumerate(chips)
        ]
        blocks = token_sem.shape[0]
        block = tokens_hbm.shape[0] // blocks
        token_copies = [
            pltpu.make_async_copy(
                tokens_hbm.at[pl.ds(at * block, block), :],
                tokens_ref.at[pl.ds(at * block, block), :],
                token_sem.at[at],
            )
            for at in range(blocks)
        ]
        weight_copies[0].start()
        token_copies[0].start()
    loads[0].wait()
    loads[1].wait()
    me = lax.axis_index("wide")
    choice = choice_ref[...]
    prompt = lax.broadcasted_iota(jnp.int32, choice.shape, 1)
    local = choice - me * owner_portion
    wanted = (mask_ref[...] == 1) & (local >= 0) & (local < owner_portion)
    top = jnp.float32(2.0**24)
    key = jnp.where(wanted, (prompt * owner_portion + local).astype(F32), top)
    copies = []
    for shift in range(wide_count):
        reader = lax.rem(me + shift, wide_count)
        low = reader * per_device
        inside = (prompt >= low) & (prompt < low + per_device)
        first = jnp.min(jnp.where(inside, key, top))
        found = jnp.where(first < top, first, 0.0).astype(jnp.int32)
        adapter = lax.rem(found, owner_portion)
        for chunk in range(CHUNKS):
            at = shift * CHUNKS + chunk
            out = messages[at]
            span = pl.ds(chunk * rows, rows)
            copies.append(
                pltpu.make_async_copy(
                    down_ref.at[adapter, span, :], out.at[:, pl.ds(0, features)], message_sem.at[2 * at]
                )
            )
            copies.append(
                pltpu.make_async_copy(
                    up_ref.at[adapter, span, :],
                    out.at[:, pl.ds(features, columns)],
                    message_sem.at[2 * at + 1],
                )
            )
    loads[2].wait()
    loads[3].wait()
    for copy in copies:
        copy.start()
    if paired:
        token_copies[1].start()
        for half in range(2):
            weight_copies[half].wait()
            for at, copy in enumerate(token_copies):
                span = pl.ds(at * block, block)
                if half == 0:
                    copy.wait()
                    if at + 2 < blocks:
                        token_copies[at + 2].start()
                    if at + 2 == blocks:
                        weight_copies[1].start()
                for out_ref, core in ((sums[2 * half], 1 - mine), (sums[2 * half + 1], mine)):
                    low = pl.multiple_of(core * columns, columns)
                    out_ref[span, :] = jnp.dot(
                        tokens_ref[span, :],
                        weight_ref[half, :, pl.ds(low, columns)],
                        preferred_element_type=F32,
                    )
    for copy in copies:
        copy.wait()


def first_step(choice, mask, down, up, tokens, weight, wide_count, per_device, paired):
    rank, features = down.shape[1:]
    columns = up.shape[2]
    row_total = tokens.shape[0]
    count = wide_count * CHUNKS
    hbm = whole_block(pl.ANY)
    operands = [choice, mask, down, up]
    scratch = [VMEM(operand.shape, operand.dtype) for operand in operands]
    scratch += [pltpu.SemaphoreType.DMA((4,)), pltpu.SemaphoreType.DMA((2 * count,))]
    out_shape = [pltpu.HBM((rank // CHUNKS, features + columns), BF16)] * count
    out_specs = [hbm] * count
    if paired:
        operands += [tokens, weight]
        out_shape += [VMEM((row_total, columns), F32)] * 4
        out_specs += [whole_block()] * 4
        scratch += [
            VMEM(tokens.shape, BF16),
            VMEM((2, features, 2 * columns), BF16),
            pltpu.SemaphoreType.DMA((4,)),
            pltpu.SemaphoreType.DMA((2,)),
        ]
    out = pl.pallas_call(
        functools.partial(first_kernel, wide_count, per_device, paired),
        out_shape=out_shape,
        in_specs=[hbm] * len(operands),
        out_specs=out_specs,
        scratch_shapes=scratch,
        compiler_params=pltpu.CompilerParams(vmem_limit_bytes=LIMIT),
        cost_estimate=SMALL,
        name="first_step",
    )(*[in_hbm(operand) for operand in operands])
    return [out[shift * CHUNKS : (shift + 1) * CHUNKS] for shift in range(wide_count)], out[count:]


def code_kernel(keep_ref, arrived_ref, code_ref, size_ref):
    block = 128
    for at in range(keep_ref.shape[0] // block):
        span = pl.ds(at * block, block)
        total = keep_ref[span, :] + arrived_ref[span, :]
        size = jnp.max(jnp.abs(total), axis=1, keepdims=True)
        inverse = jnp.where(size > 0, 1.0 / size, 0.0)
        code_ref[span, :] = jnp.round(total * inverse * STEPS).astype(jnp.int32).astype(jnp.int16)
        size_ref[pl.ds(at, 1), :] = jnp.broadcast_to(size, (block, block)).T[:1, :]


def code_rows(keep, arrived):
    row_total, columns = keep.shape
    return pl.pallas_call(
        code_kernel,
        out_shape=[
            jax.ShapeDtypeStruct((row_total, columns), jnp.int16),
            jax.ShapeDtypeStruct((row_total // 128, 128), F32),
        ],
        in_specs=[whole_block()] * 2,
        out_specs=[whole_block()] * 2,
        compiler_params=pltpu.CompilerParams(vmem_limit_bytes=LIMIT),
        cost_estimate=SMALL,
        name="code_rows",
    )(keep, arrived)


def base_kernel(keep_ref, arrived_ref, code_ref, size_ref, tokens_hbm, out_ref, tokens_ref, token_sem):
    copy = pltpu.make_async_copy(tokens_hbm, tokens_ref, token_sem)
    copy.start()
    block = 128
    columns = out_ref.shape[1]
    for at in range(keep_ref.shape[0] // block):
        span = pl.ds(at * block, block)
        size = jnp.broadcast_to(size_ref[pl.ds(at, 1), :], (block, block)).T * (1.0 / STEPS)
        size = jnp.concatenate([size] * (columns // block), axis=1)
        crossed = code_ref[span, :].astype(jnp.int32).astype(F32) * size
        out_ref[span, :] = keep_ref[span, :] + arrived_ref[span, :] + crossed
    copy.wait()


def base_rows(keep, arrived, code, size, tokens):
    return pl.pallas_call(
        base_kernel,
        out_shape=[VMEM(keep.shape, F32), VMEM(tokens.shape, BF16)],
        in_specs=[whole_block()] * 4 + [whole_block(pl.ANY)],
        out_specs=[whole_block()] * 2,
        scratch_shapes=[pltpu.SemaphoreType.DMA],
        compiler_params=pltpu.CompilerParams(vmem_limit_bytes=LIMIT),
        cost_estimate=SMALL,
        name="base_rows",
    )(keep, arrived, code, size, in_hbm(tokens))


def shrink_kernel(tokens_ref, chosen_ref, *refs):
    messages, out_ref, stacked = refs[:-3], refs[-2], refs[-1]
    rows = out_ref.shape[0]
    row_total, features = tokens_ref.shape
    block = 256
    for at, message in enumerate(messages):
        stacked[pl.ds(at * rows, rows), :] = message[:, :features]
    for low in range(0, row_total, block):
        sums = lax.dot_general(
            tokens_ref[pl.ds(low, block), :],
            stacked[...],
            (((1,), (1,)), ((), ())),
            preferred_element_type=F32,
        ).T
        total = None
        for at in range(len(messages)):
            asked = chosen_ref[pl.ds(at, 1), pl.ds(low, block)] > 0
            term = jnp.where(asked, sums[at * rows : (at + 1) * rows, :], 0.0)
            total = term if total is None else total + term
        out_ref[:, pl.ds(low, block)] = total


def shrink(tokens, chosen, messages, earlier):
    row_total, features = tokens.shape
    count = len(messages)
    rows = messages[0].shape[0]
    return pl.pallas_call(
        shrink_kernel,
        out_shape=jax.ShapeDtypeStruct((rows, row_total), F32),
        in_specs=[whole_block()] * (2 + count) + [whole_block(pl.ANY)],
        out_specs=whole_block(),
        scratch_shapes=[VMEM((count * rows, features), BF16)],
        compiler_params=pltpu.CompilerParams(vmem_limit_bytes=LIMIT),
        cost_estimate=SMALL,
        name="shrink",
    )(tokens, chosen, *messages, earlier)


def lift_kernel(base_count, part_count, features, masked, length_ref, chosen_ref, *refs):
    bases = refs[:base_count]
    parts = refs[base_count : base_count + part_count]
    messages, out_ref, stacked = refs[base_count + part_count : -2], refs[-2], refs[-1]
    rows = parts[0].shape[0]
    count = len(messages)
    half = count * rows
    for at, message in enumerate(messages):
        factor = message[:, features:]
        stacked[pl.ds(at * rows, rows), :] = factor
        stacked[pl.ds(half + at * rows, rows), :] = factor
    row_total, columns = out_ref.shape
    block = 256
    position = lax.broadcasted_iota(jnp.int32, (LEN, columns), 0)
    for low in range(0, row_total, block):
        span = pl.ds(low, block)
        shrunk = parts[0][:, span]
        for part in parts[1:]:
            shrunk = shrunk + part[:, span]
        spread = jnp.concatenate(
            [jnp.where(chosen_ref[pl.ds(at, 1), span] > 0, shrunk, 0.0) for at in range(count)], axis=0
        )
        high = spread.astype(BF16)
        remainder = (spread - high.astype(F32)).astype(BF16)
        both = jnp.concatenate([high, remainder], axis=0)
        total = lax.dot_general(
            both, stacked[...], (((0,), (0,)), ((), ())), preferred_element_type=F32
        )
        for base in bases:
            total = total + base[span, :]
        if not masked:
            out_ref[span, :] = total
            continue
        for prompt in range(block // LEN):
            piece = total[prompt * LEN : (prompt + 1) * LEN, :]
            live = position < length_ref[low // LEN + prompt]
            out_ref[pl.ds(low + prompt * LEN, LEN), :] = jnp.where(live, piece, 0.0).astype(BF16)


def lift(lengths, chosen, bases, parts, messages, features, masked):
    row_total, columns = bases[0].shape
    count = len(messages)
    rows = messages[0].shape[0]
    return pl.pallas_call(
        functools.partial(lift_kernel, len(bases), len(parts), features, masked),
        out_shape=jax.ShapeDtypeStruct((row_total, columns), BF16 if masked else F32),
        in_specs=[whole_block(pltpu.SMEM)] + [whole_block()] * (1 + len(bases) + len(parts) + count),
        out_specs=whole_block(),
        scratch_shapes=[VMEM((2 * count * rows, columns), BF16)],
        compiler_params=pltpu.CompilerParams(vmem_limit_bytes=LIMIT),
        cost_estimate=SMALL,
        name="finish" if masked else "lift",
    )(lengths, chosen, *bases, *parts, *messages)


def on_device(
    tokens,
    value_weight,
    adapter_down_factors,
    adapter_up_factors,
    adapter_choice_index,
    adapter_mask,
    prompt_token_length,
):
    wide_count = lax.axis_size("wide")
    narrow_count = lax.axis_size("narrow")
    wide_at = lax.axis_index("wide")
    owner_portion = adapter_down_factors.shape[0]
    row_total, features = tokens.shape
    per_device = row_total // LEN
    columns = adapter_up_factors.shape[2]

    paired = narrow_count == 4
    sent, sums = first_step(
        adapter_choice_index.reshape(1, -1),
        adapter_mask.reshape(1, -1),
        jnp.swapaxes(adapter_down_factors, 1, 2),
        adapter_up_factors,
        tokens,
        value_weight,
        wide_count,
        per_device,
        paired,
    )
    held = [[sent[0][chunk]] for chunk in range(CHUNKS)]
    for chunk in range(CHUNKS):
        for shift in range(1, wide_count):
            ring = [(at, (at + shift) % wide_count) for at in range(wide_count)]
            held[chunk].append(lax.ppermute(sent[shift][chunk], "wide", ring))

    my_choice = lax.dynamic_slice_in_dim(adapter_choice_index, wide_at * per_device, per_device)
    my_mask = lax.dynamic_slice_in_dim(adapter_mask, wide_at * per_device, per_device)
    my_lengths = lax.dynamic_slice_in_dim(prompt_token_length, wide_at * per_device, per_device)
    owners = (wide_at - jnp.arange(wide_count, dtype=jnp.int32) + wide_count) % wide_count
    local = my_choice[None, :] - owners[:, None] * owner_portion
    matches = (my_mask[None, :] == 1) & (local >= 0) & (local < owner_portion)
    order = jnp.arange(per_device, dtype=jnp.int32)[None, :]
    first = jnp.min(
        jnp.where(matches, order * owner_portion + local, per_device * owner_portion), axis=1
    )
    granted = first % owner_portion
    chosen_prompt = (matches & (local == granted[:, None])).astype(F32)
    chosen = jnp.repeat(chosen_prompt, LEN, axis=1)

    if paired:
        core = [(at, at ^ 1) for at in range(4)]
        across = [(at, at ^ 2) for at in range(4)]
        far_send, far_keep, near_send, near_keep = sums
        code, size = code_rows(far_keep, lax.ppermute(far_send, "narrow", core))
        base, resident = base_rows(
            near_keep,
            lax.ppermute(near_send, "narrow", core),
            lax.ppermute(code, "narrow", across),
            lax.ppermute(size, "narrow", across),
            tokens,
        )
    else:
        partial_value = jnp.dot(tokens, value_weight, preferred_element_type=F32)
        base = lax.psum_scatter(partial_value, "narrow", scatter_dimension=1, tiled=True)
        resident = tokens

    early = [base]
    for chunk in range(CHUNKS):
        part = shrink(resident, chosen, held[chunk], early[0])
        if paired:
            part = part + lax.ppermute(part, "narrow", core)
            parts = [part, lax.ppermute(part, "narrow", across)]
        else:
            parts = [lax.psum(part, "narrow")]
        last = chunk == CHUNKS - 1
        early = [lift(my_lengths, chosen, early, parts, held[chunk], features, last)]
    return early[0]


def solution(mesh):
    placed = (
        P(("groups", "wide"), "narrow"),
        P("narrow", None),
        P(("groups", "wide"), "narrow", None),
        P(("groups", "wide"), None, "narrow"),
        P("groups"),
        P("groups"),
        P("groups"),
    )
    return jax.shard_map(
        on_device,
        mesh=mesh,
        in_specs=placed,
        out_specs=P(("groups", "wide"), "narrow"),
        check_vma=False,
    )
```

```python
import functools
import math

import jax
import jax.numpy as jnp
from jax import lax
from jax.experimental import pallas as pl
from jax.experimental.pallas import tpu as pltpu
from jax.sharding import PartitionSpec as P

LEN = 32
CHUNKS = 1
LIMIT = 24 * 2**20
VMEM = pltpu.VMEM
F32 = jnp.float32
BF16 = jnp.bfloat16
STEPS = 32767.0
GRADES = 128.0
SMALL = pl.CostEstimate(flops=1, bytes_accessed=1, transcendentals=0)


def whole_block(array_memory=VMEM):
    return pl.BlockSpec(memory_space=array_memory)


def in_hbm(array):
    return pltpu.with_memory_space_constraint(array, pltpu.HBM)


def quarter_copies(weight_hbm, weight_ref, weight_sem, quarters):
    columns = weight_ref.shape[2]
    return [
        pltpu.make_async_copy(
            weight_hbm.at[:, pl.ds(pl.multiple_of(quarter * columns, columns), columns)],
            weight_ref.at[at],
            weight_sem.at[at],
        )
        for at, quarter in enumerate(quarters)
    ]


def first_kernel(wide_count, per_device, paired, *refs):
    message_count = wide_count * CHUNKS
    loads_in, refs = refs[:4], refs[4:]
    if paired:
        tokens_hbm, weight_hbm, *refs = refs
    messages, refs = refs[:message_count], refs[message_count:]
    if paired:
        sums, refs = refs[:2], refs[2:]
    choice_ref, mask_ref, down_ref, up_ref, load_sem, message_sem = refs[:6]
    owner_portion, rank, features = down_ref.shape
    columns = up_ref.shape[2]
    rows = rank // CHUNKS
    loads = [
        pltpu.make_async_copy(source, target, load_sem.at[at])
        for at, (source, target) in enumerate(zip(loads_in, refs[:4]))
    ]
    for copy in loads:
        copy.start()
    if paired:
        tokens_ref, weight_ref, send_ref, token_sem, weight_sem, send_sem = refs[6:]
        narrow_at = lax.axis_index("narrow")
        mine = lax.rem(narrow_at, 2)
        chip = 2 * (narrow_at // 2)
        weight_copies = quarter_copies(
            weight_hbm, weight_ref, weight_sem, (2 - chip + 1 - mine, 2 - chip + mine)
        )
        blocks = token_sem.shape[0]
        block = tokens_hbm.shape[0] // blocks
        token_copies = [
            pltpu.make_async_copy(
                tokens_hbm.at[pl.ds(at * block, block), :],
                tokens_ref.at[pl.ds(at * block, block), :],
                token_sem.at[at],
            )
            for at in range(blocks)
        ]
        weight_copies[0].start()
        token_copies[0].start()
    loads[0].wait()
    loads[1].wait()
    me = lax.axis_index("wide")
    choice = choice_ref[...]
    prompt = lax.broadcasted_iota(jnp.int32, choice.shape, 1)
    local = choice - me * owner_portion
    wanted = (mask_ref[...] == 1) & (local >= 0) & (local < owner_portion)
    top = jnp.float32(2.0**24)
    key = jnp.where(wanted, (prompt * owner_portion + local).astype(F32), top)
    copies = []
    for shift in range(wide_count):
        reader = lax.rem(me + shift, wide_count)
        low = reader * per_device
        inside = (prompt >= low) & (prompt < low + per_device)
        first = jnp.min(jnp.where(inside, key, top))
        found = jnp.where(first < top, first, 0.0).astype(jnp.int32)
        adapter = lax.rem(found, owner_portion)
        for chunk in range(CHUNKS):
            at = shift * CHUNKS + chunk
            out = messages[at]
            span = pl.ds(chunk * rows, rows)
            copies.append(
                pltpu.make_async_copy(
                    down_ref.at[adapter, span, :], out.at[:, pl.ds(0, features)], message_sem.at[2 * at]
                )
            )
            copies.append(
                pltpu.make_async_copy(
                    up_ref.at[adapter, span, :],
                    out.at[:, pl.ds(features, columns)],
                    message_sem.at[2 * at + 1],
                )
            )
    loads[2].wait()
    loads[3].wait()
    for copy in copies:
        copy.start()
    if paired:
        weight_copies[1].start()
        for copy in token_copies[1:]:
            copy.start()
        weight_copies[0].wait()
        for at, copy in enumerate(token_copies):
            copy.wait()
            span = pl.ds(at * block, block)
            send_ref[span, :] = jnp.dot(tokens_ref[span, :], weight_ref[0], preferred_element_type=F32)
            copy = pltpu.make_async_copy(send_ref.at[span, :], sums[0].at[span, :], send_sem.at[at])
            copy.start()
            copies.append(copy)
        weight_copies[1].wait()
        for at in range(blocks):
            span = pl.ds(at * block, block)
            sums[1][span, :] = jnp.dot(tokens_ref[span, :], weight_ref[1], preferred_element_type=F32)
    for copy in copies:
        copy.wait()


def first_step(choice, mask, down, up, tokens, weight, wide_count, per_device, paired):
    rank, features = down.shape[1:]
    columns = up.shape[2]
    row_total = tokens.shape[0]
    count = wide_count * CHUNKS
    hbm = whole_block(pl.ANY)
    operands = [choice, mask, down, up]
    scratch = [VMEM(operand.shape, operand.dtype) for operand in operands]
    scratch += [pltpu.SemaphoreType.DMA((4,)), pltpu.SemaphoreType.DMA((2 * count,))]
    out_shape = [pltpu.HBM((rank // CHUNKS, features + columns), BF16)] * count
    out_specs = [hbm] * count
    if paired:
        operands += [tokens, weight]
        out_shape += [pltpu.HBM((row_total, columns), F32), VMEM((row_total, columns), F32)]
        out_specs += [hbm, whole_block()]
        scratch += [
            VMEM(tokens.shape, BF16),
            VMEM((2, features, columns), BF16),
            VMEM((row_total, columns), F32),
            pltpu.SemaphoreType.DMA((4,)),
            pltpu.SemaphoreType.DMA((2,)),
            pltpu.SemaphoreType.DMA((4,)),
        ]
    out = pl.pallas_call(
        functools.partial(first_kernel, wide_count, per_device, paired),
        out_shape=out_shape,
        in_specs=[hbm] * len(operands),
        out_specs=out_specs,
        scratch_shapes=scratch,
        compiler_params=pltpu.CompilerParams(vmem_limit_bytes=LIMIT),
        cost_estimate=SMALL,
        name="first_step",
    )(*[in_hbm(operand) for operand in operands])
    return [out[shift * CHUNKS : (shift + 1) * CHUNKS] for shift in range(wide_count)], out[count:]


def code_kernel(keep_ref, arrived_ref, code_ref):
    block = 128
    row_total, columns = keep_ref.shape
    grades = []
    for at in range(row_total // block):
        span = pl.ds(at * block, block)
        total = keep_ref[span, :] + arrived_ref[span, :]
        size = jnp.max(jnp.abs(total), axis=1, keepdims=True)
        grade = jnp.ceil(jnp.log(jnp.maximum(size, 2.0**-120)) * (GRADES / math.log(2.0)))
        scaled = total * jnp.exp2(grade * (-1.0 / GRADES)) * STEPS
        scaled = jnp.clip(jnp.round(scaled), -STEPS, STEPS)
        code_ref[span, :] = scaled.astype(jnp.int32).astype(jnp.int16)
        grades.append(jnp.broadcast_to(grade, (block, block)).T[:1, :])
    grades = jnp.concatenate(grades + [jnp.zeros((16 - len(grades), block), F32)], axis=0)
    grades = jnp.concatenate([grades, jnp.zeros((16, columns - block), F32)], axis=1)
    code_ref[pl.ds(row_total, 16), :] = grades.astype(jnp.int32).astype(jnp.int16)


def code_rows(keep, arrived):
    row_total, columns = keep.shape
    return pl.pallas_call(
        code_kernel,
        out_shape=jax.ShapeDtypeStruct((row_total + 16, columns), jnp.int16),
        in_specs=[whole_block()] * 2,
        out_specs=whole_block(),
        compiler_params=pltpu.CompilerParams(vmem_limit_bytes=LIMIT),
        cost_estimate=SMALL,
        name="code_rows",
    )(keep, arrived)


def near_kernel(tokens_hbm, weight_hbm, ticket_ref, send_hbm, keep_ref, *scratch):
    tokens_ref, weight_ref, send_ref, token_sem, weight_sem, send_sem = scratch
    narrow_at = lax.axis_index("narrow")
    mine = lax.rem(narrow_at, 2)
    chip = 2 * (narrow_at // 2)
    weight_copies = quarter_copies(weight_hbm, weight_ref, weight_sem, (chip + 1 - mine, chip + mine))
    token_copy = pltpu.make_async_copy(tokens_hbm, tokens_ref, token_sem)
    weight_copies[0].start()
    token_copy.start()
    weight_copies[1].start()
    weight_copies[0].wait()
    token_copy.wait()
    block = 256
    spans = [pl.ds(low, block) for low in range(0, tokens_ref.shape[0], block)]
    for span in spans:
        send_ref[span, :] = jnp.dot(tokens_ref[span, :], weight_ref[0], preferred_element_type=F32)
    send_copy = pltpu.make_async_copy(send_ref, send_hbm, send_sem)
    send_copy.start()
    weight_copies[1].wait()
    for span in spans:
        keep_ref[span, :] = jnp.dot(tokens_ref[span, :], weight_ref[1], preferred_element_type=F32)
    send_copy.wait()


def near_columns(tokens, weight, ticket, columns):
    row_total, features = tokens.shape
    hbm = whole_block(pl.ANY)
    return pl.pallas_call(
        near_kernel,
        out_shape=[
            pltpu.HBM((row_total, columns), F32),
            VMEM((row_total, columns), F32),
        ],
        in_specs=[hbm] * 3,
        out_specs=[hbm, whole_block()],
        scratch_shapes=[
            VMEM(tokens.shape, BF16),
            VMEM((2, features, columns), BF16),
            VMEM((row_total, columns), F32),
            pltpu.SemaphoreType.DMA,
            pltpu.SemaphoreType.DMA((2,)),
            pltpu.SemaphoreType.DMA,
        ],
        compiler_params=pltpu.CompilerParams(vmem_limit_bytes=LIMIT),
        cost_estimate=SMALL,
        name="near_columns",
    )(in_hbm(tokens), in_hbm(weight), ticket)


def reload_kernel(tokens_hbm, ticket_ref, tokens_ref, token_sem):
    copy = pltpu.make_async_copy(tokens_hbm, tokens_ref, token_sem)
    copy.start()
    copy.wait()


def reload_tokens(tokens, ticket):
    return pl.pallas_call(
        reload_kernel,
        out_shape=VMEM(tokens.shape, BF16),
        in_specs=[whole_block(pl.ANY)] * 2,
        out_specs=whole_block(),
        scratch_shapes=[pltpu.SemaphoreType.DMA],
        compiler_params=pltpu.CompilerParams(vmem_limit_bytes=LIMIT),
        cost_estimate=SMALL,
        name="reload_tokens",
    )(in_hbm(tokens), ticket)


def base_kernel(keep_ref, arrived_ref, code_ref, out_ref):
    row_total, columns = out_ref.shape
    block = 128
    grades = code_ref[pl.ds(row_total, 16), :].astype(jnp.int32).astype(F32)
    sizes = jnp.exp2(grades[:, :block] * (1.0 / GRADES)) * (1.0 / STEPS)
    for at in range(row_total // block):
        span = pl.ds(at * block, block)
        size = jnp.broadcast_to(sizes[at : at + 1, :], (block, block)).T
        size = jnp.concatenate([size] * (columns // block), axis=1)
        crossed = code_ref[span, :].astype(jnp.int32).astype(F32) * size
        out_ref[span, :] = keep_ref[span, :] + arrived_ref[span, :] + crossed


def base_rows(keep, arrived, code):
    return pl.pallas_call(
        base_kernel,
        out_shape=VMEM(keep.shape, F32),
        in_specs=[whole_block()] * 3,
        out_specs=whole_block(),
        compiler_params=pltpu.CompilerParams(vmem_limit_bytes=LIMIT),
        cost_estimate=SMALL,
        name="base_rows",
    )(keep, arrived, code)


def row_parts(refs):
    if len(refs) == 1:
        return [(refs[0], 0)]
    mine = lax.rem(lax.axis_index("narrow"), 2)
    length = refs[0].shape[1]
    return [(refs[0], mine * length), (refs[1], (1 - mine) * length)]


def shrink_kernel(part_count, tokens_ref, chosen_ref, *refs):
    messages, outs, stacked = refs[: -part_count - 1], refs[-part_count - 1 : -1], refs[-1]
    rows = outs[0].shape[0]
    features = tokens_ref.shape[1]
    block = 256
    for at, message in enumerate(messages):
        stacked[pl.ds(at * rows, rows), :] = message[:, :features]
    for out_ref, start in row_parts(outs)[::-1]:
        for low in range(0, out_ref.shape[1], block):
            span = pl.ds(pl.multiple_of(start + low, block), block)
            sums = lax.dot_general(
                tokens_ref[span, :], stacked[...], (((1,), (1,)), ((), ())), preferred_element_type=F32
            ).T
            asked = chosen_ref[:, span] > 0
            total = None
            for at in range(len(messages)):
                term = jnp.where(asked[at : at + 1, :], sums[at * rows : (at + 1) * rows, :], 0.0)
                total = term if total is None else total + term
            out_ref[:, pl.ds(low, block)] = total


def shrink(tokens, chosen, messages, part_count):
    row_total, features = tokens.shape
    count = len(messages)
    rows = messages[0].shape[0]
    return pl.pallas_call(
        functools.partial(shrink_kernel, part_count),
        out_shape=[jax.ShapeDtypeStruct((rows, row_total // part_count), F32)] * part_count,
        in_specs=[whole_block()] * (2 + count),
        out_specs=[whole_block()] * part_count,
        scratch_shapes=[VMEM((count * rows, features), BF16)],
        compiler_params=pltpu.CompilerParams(vmem_limit_bytes=LIMIT),
        cost_estimate=SMALL,
        name="shrink",
    )(tokens, chosen, *messages)


def finish_kernel(part_count, features, length_ref, chosen_ref, *refs):
    base_ref, refs = refs[0], refs[1:]
    parts = refs[:part_count]
    messages, out_ref, stacked = refs[part_count:-2], refs[-2], refs[-1]
    rows = parts[0].shape[0]
    count = len(messages)
    half = count * rows
    for at, message in enumerate(messages):
        factor = message[:, features:]
        stacked[pl.ds(at * rows, rows), :] = factor
        stacked[pl.ds(half + at * rows, rows), :] = factor
    columns = out_ref.shape[1]
    block = 256
    position = lax.broadcasted_iota(jnp.int32, (LEN, columns), 0)
    for part_ref, start in row_parts(parts):
        for low in range(0, part_ref.shape[1], block):
            first_row = pl.multiple_of(start + low, block)
            span = pl.ds(first_row, block)
            shrunk = part_ref[:, pl.ds(low, block)]
            asked = chosen_ref[:, span] > 0
            spread = jnp.concatenate(
                [jnp.where(asked[at : at + 1, :], shrunk, 0.0) for at in range(count)], axis=0
            )
            high = spread.astype(BF16)
            remainder = (spread - high.astype(F32)).astype(BF16)
            both = jnp.concatenate([high, remainder], axis=0)
            total = base_ref[span, :] + lax.dot_general(
                both, stacked[...], (((0,), (0,)), ((), ())), preferred_element_type=F32
            )
            for prompt in range(block // LEN):
                piece = total[prompt * LEN : (prompt + 1) * LEN, :]
                live = position < length_ref[first_row // LEN + prompt]
                rows_at = pl.ds(pl.multiple_of(first_row + prompt * LEN, LEN), LEN)
                out_ref[rows_at, :] = jnp.where(live, piece, 0.0).astype(BF16)


def finish(lengths, chosen, base, parts, messages, features):
    row_total, columns = base.shape
    count = len(messages)
    rows = messages[0].shape[0]
    operands = [chosen, base, *parts, *messages]
    return pl.pallas_call(
        functools.partial(finish_kernel, len(parts), features),
        out_shape=jax.ShapeDtypeStruct((row_total, columns), BF16),
        in_specs=[whole_block(pltpu.SMEM)] + [whole_block()] * len(operands),
        out_specs=whole_block(),
        scratch_shapes=[VMEM((2 * count * rows, columns), BF16)],
        compiler_params=pltpu.CompilerParams(vmem_limit_bytes=LIMIT),
        cost_estimate=SMALL,
        name="finish",
    )(lengths, *operands)


def on_device(
    tokens,
    value_weight,
    adapter_down_factors,
    adapter_up_factors,
    adapter_choice_index,
    adapter_mask,
    prompt_token_length,
):
    wide_count = lax.axis_size("wide")
    narrow_count = lax.axis_size("narrow")
    wide_at = lax.axis_index("wide")
    owner_portion = adapter_down_factors.shape[0]
    row_total, features = tokens.shape
    per_device = row_total // LEN
    columns = adapter_up_factors.shape[2]

    paired = narrow_count == 4
    sent, sums = first_step(
        adapter_choice_index.reshape(1, -1),
        adapter_mask.reshape(1, -1),
        jnp.swapaxes(adapter_down_factors, 1, 2),
        adapter_up_factors,
        tokens,
        value_weight,
        wide_count,
        per_device,
        paired,
    )
    held = [[sent[0][chunk]] for chunk in range(CHUNKS)]
    for chunk in range(CHUNKS):
        for shift in range(1, wide_count):
            ring = [(at, (at + shift) % wide_count) for at in range(wide_count)]
            held[chunk].append(lax.ppermute(sent[shift][chunk], "wide", ring))

    my_choice = lax.dynamic_slice_in_dim(adapter_choice_index, wide_at * per_device, per_device)
    my_mask = lax.dynamic_slice_in_dim(adapter_mask, wide_at * per_device, per_device)
    my_lengths = lax.dynamic_slice_in_dim(prompt_token_length, wide_at * per_device, per_device)
    owners = (wide_at - jnp.arange(wide_count, dtype=jnp.int32) + wide_count) % wide_count
    local = my_choice[None, :] - owners[:, None] * owner_portion
    matches = (my_mask[None, :] == 1) & (local >= 0) & (local < owner_portion)
    order = jnp.arange(per_device, dtype=jnp.int32)[None, :]
    first = jnp.min(
        jnp.where(matches, order * owner_portion + local, per_device * owner_portion), axis=1
    )
    granted = first % owner_portion
    chosen_prompt = (matches & (local == granted[:, None])).astype(F32)
    chosen = jnp.repeat(chosen_prompt, LEN, axis=1)

    if paired:
        core = [(at, at ^ 1) for at in range(4)]
        across = [(at, at ^ 2) for at in range(4)]
        far_send, far_keep = sums
        code = code_rows(far_keep, lax.ppermute(far_send, "narrow", core))
        near_send, near_keep = near_columns(tokens, value_weight, code, columns)
        resident = reload_tokens(tokens, near_keep)
        base = base_rows(
            near_keep, lax.ppermute(near_send, "narrow", core), lax.ppermute(code, "narrow", across)
        )
        keep, send = shrink(resident, chosen, held[0], 2)
        part = keep + lax.ppermute(send, "narrow", core)
        part = part + lax.ppermute(part, "narrow", across)
        parts = [part, lax.ppermute(part, "narrow", core)]
    else:
        partial_value = jnp.dot(tokens, value_weight, preferred_element_type=F32)
        base = lax.psum_scatter(partial_value, "narrow", scatter_dimension=1, tiled=True)
        parts = [lax.psum(shrink(tokens, chosen, held[0], 1)[0], "narrow")]
    return finish(my_lengths, chosen, base, parts, held[0], features)


def solution(mesh):
    placed = (
        P(("groups", "wide"), "narrow"),
        P("narrow", None),
        P(("groups", "wide"), "narrow", None),
        P(("groups", "wide"), None, "narrow"),
        P("groups"),
        P("groups"),
        P("groups"),
    )
    return jax.shard_map(
        on_device,
        mesh=mesh,
        in_specs=placed,
        out_specs=P(("groups", "wide"), "narrow"),
        check_vma=False,
    )
```

```python
import functools
import math

import jax
import jax.numpy as jnp
from jax import lax
from jax.experimental import pallas as pl
from jax.experimental.pallas import tpu as pltpu
from jax.sharding import PartitionSpec as P

LEN = 32
CHUNKS = 1
LIMIT = 24 * 2**20
VMEM = pltpu.VMEM
F32 = jnp.float32
BF16 = jnp.bfloat16
STEPS = 32767.0
GRADES = 128.0
SMALL = pl.CostEstimate(flops=1, bytes_accessed=1, transcendentals=0)


def whole_block(array_memory=VMEM):
    return pl.BlockSpec(memory_space=array_memory)


def in_hbm(array):
    return pltpu.with_memory_space_constraint(array, pltpu.HBM)


def quarter_copies(weight_hbm, weight_ref, weight_sem, quarters):
    columns = weight_ref.shape[2]
    return [
        pltpu.make_async_copy(
            weight_hbm.at[:, pl.ds(pl.multiple_of(quarter * columns, columns), columns)],
            weight_ref.at[at],
            weight_sem.at[at],
        )
        for at, quarter in enumerate(quarters)
    ]


def pack_kernel(wide_count, per_device, *refs):
    message_count = wide_count * CHUNKS
    loads_in, refs = refs[:4], refs[4:]
    messages, refs = refs[:message_count], refs[message_count:]
    ticket_ref, refs = refs[0], refs[1:]
    ticket_ref[...] = jnp.zeros_like(ticket_ref)
    choice_ref, mask_ref, down_ref, up_ref, load_sem, message_sem = refs[:6]
    owner_portion, rank, features = down_ref.shape
    columns = up_ref.shape[2]
    rows = rank // CHUNKS
    loads = [
        pltpu.make_async_copy(source, target, load_sem.at[at])
        for at, (source, target) in enumerate(zip(loads_in, refs[:4]))
    ]
    for copy in loads:
        copy.start()
    loads[0].wait()
    loads[1].wait()
    me = lax.axis_index("wide")
    choice = choice_ref[...]
    prompt = lax.broadcasted_iota(jnp.int32, choice.shape, 1)
    local = choice - me * owner_portion
    wanted = (mask_ref[...] == 1) & (local >= 0) & (local < owner_portion)
    top = jnp.float32(2.0**24)
    key = jnp.where(wanted, (prompt * owner_portion + local).astype(F32), top)
    copies = []
    for shift in range(wide_count):
        reader = lax.rem(me + shift, wide_count)
        low = reader * per_device
        inside = (prompt >= low) & (prompt < low + per_device)
        first = jnp.min(jnp.where(inside, key, top))
        found = jnp.where(first < top, first, 0.0).astype(jnp.int32)
        adapter = lax.rem(found, owner_portion)
        for chunk in range(CHUNKS):
            at = shift * CHUNKS + chunk
            out = messages[at]
            span = pl.ds(chunk * rows, rows)
            copies.append(
                pltpu.make_async_copy(
                    down_ref.at[adapter, span, :], out.at[:, pl.ds(0, features)], message_sem.at[2 * at]
                )
            )
            copies.append(
                pltpu.make_async_copy(
                    up_ref.at[adapter, span, :],
                    out.at[:, pl.ds(features, columns)],
                    message_sem.at[2 * at + 1],
                )
            )
    loads[2].wait()
    loads[3].wait()
    for copy in copies:
        copy.start()
    for copy in copies:
        copy.wait()


def pack_messages(choice, mask, down, up, wide_count, per_device):
    rank, features = down.shape[1:]
    columns = up.shape[2]
    count = wide_count * CHUNKS
    hbm = whole_block(pl.ANY)
    operands = [choice, mask, down, up]
    scratch = [VMEM(operand.shape, operand.dtype) for operand in operands]
    scratch += [pltpu.SemaphoreType.DMA((4,)), pltpu.SemaphoreType.DMA((2 * count,))]
    out_shape = [pltpu.HBM((rank // CHUNKS, features + columns), BF16)] * count
    out_specs = [hbm] * count + [whole_block()]
    out_shape += [jax.ShapeDtypeStruct((8, 128), F32)]
    out = pl.pallas_call(
        functools.partial(pack_kernel, wide_count, per_device),
        out_shape=out_shape,
        in_specs=[hbm] * len(operands),
        out_specs=out_specs,
        scratch_shapes=scratch,
        compiler_params=pltpu.CompilerParams(vmem_limit_bytes=LIMIT),
        cost_estimate=SMALL,
        name="pack_messages",
    )(*[in_hbm(operand) for operand in operands])
    return [out[shift * CHUNKS : (shift + 1) * CHUNKS] for shift in range(wide_count)], out[-1]


def code_kernel(keep_ref, arrived_ref, code_ref):
    block = 128
    row_total, columns = keep_ref.shape
    grades = []
    for at in range(row_total // block):
        span = pl.ds(at * block, block)
        total = keep_ref[span, :] + arrived_ref[span, :]
        size = jnp.max(jnp.abs(total), axis=1, keepdims=True)
        grade = jnp.ceil(jnp.log(jnp.maximum(size, 2.0**-120)) * (GRADES / math.log(2.0)))
        scaled = total * jnp.exp2(grade * (-1.0 / GRADES)) * STEPS
        scaled = jnp.clip(jnp.round(scaled), -STEPS, STEPS)
        code_ref[span, :] = scaled.astype(jnp.int32).astype(jnp.int16)
        grades.append(jnp.broadcast_to(grade, (block, block)).T[:1, :])
    grades = jnp.concatenate(grades + [jnp.zeros((16 - len(grades), block), F32)], axis=0)
    grades = jnp.concatenate([grades, jnp.zeros((16, columns - block), F32)], axis=1)
    code_ref[pl.ds(row_total, 16), :] = grades.astype(jnp.int32).astype(jnp.int16)


def code_rows(keep, arrived):
    row_total, columns = keep.shape
    return pl.pallas_call(
        code_kernel,
        out_shape=jax.ShapeDtypeStruct((row_total + 16, columns), jnp.int16),
        in_specs=[whole_block()] * 2,
        out_specs=whole_block(),
        compiler_params=pltpu.CompilerParams(vmem_limit_bytes=LIMIT),
        cost_estimate=SMALL,
        name="code_rows",
    )(keep, arrived)


def dots_kernel(flip, tokens_hbm, weight_hbm, ticket_ref, send_hbm, keep_ref, *scratch):
    tokens_ref, weight_ref, send_ref, token_sem, weight_sem, send_sem = scratch
    narrow_at = lax.axis_index("narrow")
    mine = lax.rem(narrow_at, 2)
    chip = 2 * ((narrow_at // 2) ^ flip)
    weight_copies = quarter_copies(weight_hbm, weight_ref, weight_sem, (chip + 1 - mine, chip + mine))
    blocks = token_sem.shape[0]
    block = tokens_hbm.shape[0] // blocks
    spans = [pl.ds(at * block, block) for at in range(blocks)]
    token_copies = [
        pltpu.make_async_copy(tokens_hbm.at[span, :], tokens_ref.at[span, :], token_sem.at[at])
        for at, span in enumerate(spans)
    ]
    weight_copies[0].start()
    token_copies[0].start()
    token_copies[1].start()
    weight_copies[0].wait()
    weight_copies[1].start()
    copies = []
    for at, span in enumerate(spans):
        token_copies[at].wait()
        if at + 2 < blocks:
            token_copies[at + 2].start()
        send_ref[span, :] = jnp.dot(tokens_ref[span, :], weight_ref[0], preferred_element_type=F32)
        copies.append(pltpu.make_async_copy(send_ref.at[span, :], send_hbm.at[span, :], send_sem.at[at]))
        copies[-1].start()
    weight_copies[1].wait()
    for span in spans:
        keep_ref[span, :] = jnp.dot(tokens_ref[span, :], weight_ref[1], preferred_element_type=F32)
    for copy in copies:
        copy.wait()


def column_dots(tokens, weight, ticket, columns, flip):
    row_total, features = tokens.shape
    hbm = whole_block(pl.ANY)
    return pl.pallas_call(
        functools.partial(dots_kernel, flip),
        out_shape=[pltpu.HBM((row_total, columns), F32), VMEM((row_total, columns), F32)],
        in_specs=[hbm] * 3,
        out_specs=[hbm, whole_block()],
        scratch_shapes=[
            VMEM(tokens.shape, BF16),
            VMEM((2, features, columns), BF16),
            VMEM((row_total, columns), F32),
            pltpu.SemaphoreType.DMA((4,)),
            pltpu.SemaphoreType.DMA((2,)),
            pltpu.SemaphoreType.DMA((4,)),
        ],
        compiler_params=pltpu.CompilerParams(vmem_limit_bytes=LIMIT),
        cost_estimate=pl.CostEstimate(flops=1 if flip else 10000000000, bytes_accessed=1, transcendentals=0),
        name="far_columns" if flip else "near_columns",
    )(in_hbm(tokens), in_hbm(weight), ticket)


def reload_kernel(tokens_hbm, ticket_ref, tokens_ref, token_sem):
    copy = pltpu.make_async_copy(tokens_hbm, tokens_ref, token_sem)
    copy.start()
    copy.wait()


def reload_tokens(tokens, ticket):
    return pl.pallas_call(
        reload_kernel,
        out_shape=VMEM(tokens.shape, BF16),
        in_specs=[whole_block(pl.ANY)] * 2,
        out_specs=whole_block(),
        scratch_shapes=[pltpu.SemaphoreType.DMA],
        compiler_params=pltpu.CompilerParams(vmem_limit_bytes=LIMIT),
        cost_estimate=SMALL,
        name="reload_tokens",
    )(in_hbm(tokens), ticket)


def base_kernel(keep_ref, arrived_ref, code_ref, out_ref):
    row_total, columns = out_ref.shape
    block = 128
    grades = code_ref[pl.ds(row_total, 16), :].astype(jnp.int32).astype(F32)
    sizes = jnp.exp2(grades[:, :block] * (1.0 / GRADES)) * (1.0 / STEPS)
    for at in range(row_total // block):
        span = pl.ds(at * block, block)
        size = jnp.broadcast_to(sizes[at : at + 1, :], (block, block)).T
        size = jnp.concatenate([size] * (columns // block), axis=1)
        crossed = code_ref[span, :].astype(jnp.int32).astype(F32) * size
        out_ref[span, :] = keep_ref[span, :] + arrived_ref[span, :] + crossed


def base_rows(keep, arrived, code):
    return pl.pallas_call(
        base_kernel,
        out_shape=VMEM(keep.shape, F32),
        in_specs=[whole_block()] * 3,
        out_specs=whole_block(),
        compiler_params=pltpu.CompilerParams(vmem_limit_bytes=LIMIT),
        cost_estimate=SMALL,
        name="base_rows",
    )(keep, arrived, code)


def row_parts(refs):
    if len(refs) == 1:
        return [(refs[0], 0)]
    mine = lax.rem(lax.axis_index("narrow"), 2)
    length = refs[0].shape[1]
    return [(refs[0], mine * length), (refs[1], (1 - mine) * length)]


def shrink_kernel(part_count, tokens_ref, chosen_ref, *refs):
    messages, outs, stacked = refs[: -part_count - 1], refs[-part_count - 1 : -1], refs[-1]
    rows = outs[0].shape[0]
    features = tokens_ref.shape[1]
    block = 256
    for at, message in enumerate(messages):
        stacked[pl.ds(at * rows, rows), :] = message[:, :features]
    for out_ref, start in row_parts(outs)[::-1]:
        for low in range(0, out_ref.shape[1], block):
            span = pl.ds(pl.multiple_of(start + low, block), block)
            sums = lax.dot_general(
                tokens_ref[span, :], stacked[...], (((1,), (1,)), ((), ())), preferred_element_type=F32
            ).T
            asked = chosen_ref[:, span] > 0
            total = None
            for at in range(len(messages)):
                term = jnp.where(asked[at : at + 1, :], sums[at * rows : (at + 1) * rows, :], 0.0)
                total = term if total is None else total + term
            out_ref[:, pl.ds(low, block)] = total


def shrink(tokens, chosen, messages, part_count):
    row_total, features = tokens.shape
    count = len(messages)
    rows = messages[0].shape[0]
    return pl.pallas_call(
        functools.partial(shrink_kernel, part_count),
        out_shape=[jax.ShapeDtypeStruct((rows, row_total // part_count), F32)] * part_count,
        in_specs=[whole_block()] * (2 + count),
        out_specs=[whole_block()] * part_count,
        scratch_shapes=[VMEM((count * rows, features), BF16)],
        compiler_params=pltpu.CompilerParams(vmem_limit_bytes=LIMIT),
        cost_estimate=SMALL,
        name="shrink",
    )(tokens, chosen, *messages)


def finish_kernel(part_count, features, length_ref, chosen_ref, *refs):
    base_ref, refs = refs[0], refs[1:]
    parts = refs[:part_count]
    messages, out_ref, stacked = refs[part_count:-2], refs[-2], refs[-1]
    rows = parts[0].shape[0]
    count = len(messages)
    half = count * rows
    for at, message in enumerate(messages):
        factor = message[:, features:]
        stacked[pl.ds(at * rows, rows), :] = factor
        stacked[pl.ds(half + at * rows, rows), :] = factor
    columns = out_ref.shape[1]
    block = 256
    position = lax.broadcasted_iota(jnp.int32, (LEN, columns), 0)
    for part_ref, start in row_parts(parts):
        for low in range(0, part_ref.shape[1], block):
            first_row = pl.multiple_of(start + low, block)
            span = pl.ds(first_row, block)
            shrunk = part_ref[:, pl.ds(low, block)]
            asked = chosen_ref[:, span] > 0
            spread = jnp.concatenate(
                [jnp.where(asked[at : at + 1, :], shrunk, 0.0) for at in range(count)], axis=0
            )
            high = spread.astype(BF16)
            remainder = (spread - high.astype(F32)).astype(BF16)
            both = jnp.concatenate([high, remainder], axis=0)
            total = base_ref[span, :] + lax.dot_general(
                both, stacked[...], (((0,), (0,)), ((), ())), preferred_element_type=F32
            )
            for prompt in range(block // LEN):
                piece = total[prompt * LEN : (prompt + 1) * LEN, :]
                live = position < length_ref[first_row // LEN + prompt]
                rows_at = pl.ds(pl.multiple_of(first_row + prompt * LEN, LEN), LEN)
                out_ref[rows_at, :] = jnp.where(live, piece, 0.0).astype(BF16)


def finish(lengths, chosen, base, parts, messages, features):
    row_total, columns = base.shape
    count = len(messages)
    rows = messages[0].shape[0]
    operands = [chosen, base, *parts, *messages]
    return pl.pallas_call(
        functools.partial(finish_kernel, len(parts), features),
        out_shape=jax.ShapeDtypeStruct((row_total, columns), BF16),
        in_specs=[whole_block(pltpu.SMEM)] + [whole_block()] * len(operands),
        out_specs=whole_block(),
        scratch_shapes=[VMEM((2 * count * rows, columns), BF16)],
        compiler_params=pltpu.CompilerParams(vmem_limit_bytes=LIMIT),
        cost_estimate=SMALL,
        name="finish",
    )(lengths, *operands)


def on_device(
    tokens,
    value_weight,
    adapter_down_factors,
    adapter_up_factors,
    adapter_choice_index,
    adapter_mask,
    prompt_token_length,
):
    wide_count = lax.axis_size("wide")
    narrow_count = lax.axis_size("narrow")
    wide_at = lax.axis_index("wide")
    owner_portion = adapter_down_factors.shape[0]
    row_total, features = tokens.shape
    per_device = row_total // LEN
    columns = adapter_up_factors.shape[2]

    paired = narrow_count == 4
    sent, ticket = pack_messages(
        adapter_choice_index.reshape(1, -1),
        adapter_mask.reshape(1, -1),
        jnp.swapaxes(adapter_down_factors, 1, 2),
        adapter_up_factors,
        wide_count,
        per_device,
    )
    held = [[sent[0][chunk]] for chunk in range(CHUNKS)]
    for chunk in range(CHUNKS):
        for shift in range(1, wide_count):
            ring = [(at, (at + shift) % wide_count) for at in range(wide_count)]
            held[chunk].append(lax.ppermute(sent[shift][chunk], "wide", ring))

    my_choice = lax.dynamic_slice_in_dim(adapter_choice_index, wide_at * per_device, per_device)
    my_mask = lax.dynamic_slice_in_dim(adapter_mask, wide_at * per_device, per_device)
    my_lengths = lax.dynamic_slice_in_dim(prompt_token_length, wide_at * per_device, per_device)
    owners = (wide_at - jnp.arange(wide_count, dtype=jnp.int32) + wide_count) % wide_count
    local = my_choice[None, :] - owners[:, None] * owner_portion
    matches = (my_mask[None, :] == 1) & (local >= 0) & (local < owner_portion)
    order = jnp.arange(per_device, dtype=jnp.int32)[None, :]
    first = jnp.min(
        jnp.where(matches, order * owner_portion + local, per_device * owner_portion), axis=1
    )
    granted = first % owner_portion
    chosen_prompt = (matches & (local == granted[:, None])).astype(F32)
    chosen = jnp.repeat(chosen_prompt, LEN, axis=1)

    if paired:
        core = [(at, at ^ 1) for at in range(4)]
        across = [(at, at ^ 2) for at in range(4)]
        ticket = lax.ppermute(ticket, "narrow", core)
        far_send, far_keep = column_dots(tokens, value_weight, ticket, columns, 1)
        code = code_rows(far_keep, lax.ppermute(far_send, "narrow", core))
        near_send, near_keep = column_dots(tokens, value_weight, far_keep, columns, 0)
        resident = reload_tokens(tokens, near_keep)
        base = base_rows(
            near_keep, lax.ppermute(near_send, "narrow", core), lax.ppermute(code, "narrow", across)
        )
        keep, send = shrink(resident, chosen, held[0], 2)
        part = keep + lax.ppermute(send, "narrow", core)
        part = part + lax.ppermute(part, "narrow", across)
        parts = [part, lax.ppermute(part, "narrow", core)]
    else:
        partial_value = jnp.dot(tokens, value_weight, preferred_element_type=F32)
        base = lax.psum_scatter(partial_value, "narrow", scatter_dimension=1, tiled=True)
        parts = [lax.psum(shrink(tokens, chosen, held[0], 1)[0], "narrow")]
    return finish(my_lengths, chosen, base, parts, held[0], features)


def solution(mesh):
    placed = (
        P(("groups", "wide"), "narrow"),
        P("narrow", None),
        P(("groups", "wide"), "narrow", None),
        P(("groups", "wide"), None, "narrow"),
        P("groups"),
        P("groups"),
        P("groups"),
    )
    return jax.shard_map(
        on_device,
        mesh=mesh,
        in_specs=placed,
        out_specs=P(("groups", "wide"), "narrow"),
        check_vma=False,
    )
```

```python
import functools
import math

import jax
import jax.numpy as jnp
from jax import lax
from jax.experimental import pallas as pl
from jax.experimental.pallas import tpu as pltpu
from jax.sharding import PartitionSpec as P

LEN = 32
CHUNKS = 1
LIMIT = 24 * 2**20
VMEM = pltpu.VMEM
F32 = jnp.float32
BF16 = jnp.bfloat16
STEPS = 32767.0
GRADES = 128.0
SMALL = pl.CostEstimate(flops=1, bytes_accessed=1, transcendentals=0)
LARGE = pl.CostEstimate(flops=10**10, bytes_accessed=1, transcendentals=0)


def whole_block(array_memory=VMEM):
    return pl.BlockSpec(memory_space=array_memory)


def in_hbm(array):
    return pltpu.with_memory_space_constraint(array, pltpu.HBM)


def quarter_copies(weight_hbm, weight_ref, weight_sem, quarters):
    columns = weight_ref.shape[2]
    return [
        pltpu.make_async_copy(
            weight_hbm.at[:, pl.ds(pl.multiple_of(quarter * columns, columns), columns)],
            weight_ref.at[at],
            weight_sem.at[at],
        )
        for at, quarter in enumerate(quarters)
    ]


def pack_kernel(wide_count, per_device, *refs):
    message_count = wide_count * CHUNKS
    loads_in, refs = refs[:4], refs[4:]
    messages, refs = refs[:message_count], refs[message_count:]
    ticket_ref, refs = refs[0], refs[1:]
    ticket_ref[...] = jnp.zeros_like(ticket_ref)
    choice_ref, mask_ref, down_ref, up_ref, load_sem, message_sem = refs[:6]
    owner_portion, rank, features = down_ref.shape
    columns = up_ref.shape[2]
    rows = rank // CHUNKS
    loads = [
        pltpu.make_async_copy(source, target, load_sem.at[at])
        for at, (source, target) in enumerate(zip(loads_in, refs[:4]))
    ]
    for copy in loads:
        copy.start()
    loads[0].wait()
    loads[1].wait()
    me = lax.axis_index("wide")
    choice = choice_ref[...]
    prompt = lax.broadcasted_iota(jnp.int32, choice.shape, 1)
    local = choice - me * owner_portion
    wanted = (mask_ref[...] == 1) & (local >= 0) & (local < owner_portion)
    top = jnp.float32(2.0**24)
    key = jnp.where(wanted, (prompt * owner_portion + local).astype(F32), top)
    copies = []
    for shift in range(wide_count):
        reader = lax.rem(me + shift, wide_count)
        low = reader * per_device
        inside = (prompt >= low) & (prompt < low + per_device)
        first = jnp.min(jnp.where(inside, key, top))
        found = jnp.where(first < top, first, 0.0).astype(jnp.int32)
        adapter = lax.rem(found, owner_portion)
        for chunk in range(CHUNKS):
            at = shift * CHUNKS + chunk
            out = messages[at]
            span = pl.ds(chunk * rows, rows)
            copies.append(
                pltpu.make_async_copy(
                    down_ref.at[adapter, span, :], out.at[:, pl.ds(0, features)], message_sem.at[2 * at]
                )
            )
            copies.append(
                pltpu.make_async_copy(
                    up_ref.at[adapter, span, :],
                    out.at[:, pl.ds(features, columns)],
                    message_sem.at[2 * at + 1],
                )
            )
    loads[2].wait()
    loads[3].wait()
    for copy in copies:
        copy.start()
    for copy in copies:
        copy.wait()


def pack_messages(choice, mask, down, up, wide_count, per_device):
    rank, features = down.shape[1:]
    columns = up.shape[2]
    count = wide_count * CHUNKS
    hbm = whole_block(pl.ANY)
    operands = [choice, mask, down, up]
    scratch = [VMEM(operand.shape, operand.dtype) for operand in operands]
    scratch += [pltpu.SemaphoreType.DMA((4,)), pltpu.SemaphoreType.DMA((2 * count,))]
    out_shape = [pltpu.HBM((rank // CHUNKS, features + columns), BF16)] * count
    out_specs = [hbm] * count + [whole_block()]
    out_shape += [jax.ShapeDtypeStruct((8, 128), F32)]
    out = pl.pallas_call(
        functools.partial(pack_kernel, wide_count, per_device),
        out_shape=out_shape,
        in_specs=[hbm] * len(operands),
        out_specs=out_specs,
        scratch_shapes=scratch,
        compiler_params=pltpu.CompilerParams(vmem_limit_bytes=LIMIT),
        cost_estimate=SMALL,
        name="pack_messages",
    )(*[in_hbm(operand) for operand in operands])
    return [out[shift * CHUNKS : (shift + 1) * CHUNKS] for shift in range(wide_count)], out[-1]


def grade_of(size):
    return jnp.ceil(jnp.log(jnp.maximum(size, 2.0**-120)) * (GRADES / math.log(2.0)))


def size_of(grade):
    return jnp.exp2(grade * (1.0 / GRADES)) * (1.0 / STEPS)


def coded(total, grade):
    scaled = total * jnp.exp2(grade * (-1.0 / GRADES)) * STEPS
    return jnp.clip(jnp.round(scaled), -STEPS, STEPS).astype(jnp.int32).astype(jnp.int16)


def code_kernel(keep_ref, arrived_ref, code_ref):
    block = 128
    row_total, columns = keep_ref.shape
    grades = []
    for at in range(row_total // block):
        span = pl.ds(at * block, block)
        total = keep_ref[span, :] + arrived_ref[span, :]
        grade = grade_of(jnp.max(jnp.abs(total), axis=1, keepdims=True))
        code_ref[span, :] = coded(total, grade)
        grades.append(jnp.broadcast_to(grade, (block, block)).T[:1, :])
    grades = jnp.concatenate(grades + [jnp.zeros((16 - len(grades), block), F32)], axis=0)
    grades = jnp.concatenate([grades, jnp.zeros((16, columns - block), F32)], axis=1)
    code_ref[pl.ds(row_total, 16), :] = grades.astype(jnp.int32).astype(jnp.int16)


def code_rows(keep, arrived):
    row_total, columns = keep.shape
    return pl.pallas_call(
        code_kernel,
        out_shape=jax.ShapeDtypeStruct((row_total + 16, columns), jnp.int16),
        in_specs=[whole_block()] * 2,
        out_specs=whole_block(),
        compiler_params=pltpu.CompilerParams(vmem_limit_bytes=LIMIT),
        cost_estimate=SMALL,
        name="code_rows",
    )(keep, arrived)


def pair_dots(tokens_ref, weight_ref, weight_copies, spans, ready, send_ref, keep_ref, send_hbm, send_sem):
    weight_copies[0].wait()
    copies = []
    for at, span in enumerate(spans):
        ready(at)
        send_ref[span, :] = jnp.dot(tokens_ref[span, :], weight_ref[0], preferred_element_type=F32)
        copies.append(pltpu.make_async_copy(send_ref.at[span, :], send_hbm.at[span, :], send_sem.at[at]))
        copies[-1].start()
    weight_copies[1].wait()
    for span in spans:
        keep_ref[span, :] = jnp.dot(tokens_ref[span, :], weight_ref[1], preferred_element_type=F32)
    for copy in copies:
        copy.wait()


def row_spans(row_total, blocks):
    return [pl.ds(at * (row_total // blocks), row_total // blocks) for at in range(blocks)]


def far_kernel(tokens_hbm, weight_hbm, ticket_ref, send_hbm, keep_ref, tokens_ref, *scratch):
    weight_ref, send_ref, weight_sem, send_sem, token_sem = scratch
    narrow_at = lax.axis_index("narrow")
    mine = lax.rem(narrow_at, 2)
    chip = 2 * ((narrow_at // 2) ^ 1)
    weight_copies = quarter_copies(weight_hbm, weight_ref, weight_sem, (chip + 1 - mine, chip + mine))
    blocks = token_sem.shape[0]
    spans = row_spans(tokens_hbm.shape[0], blocks)
    token_copies = [
        pltpu.make_async_copy(tokens_hbm.at[span, :], tokens_ref.at[span, :], token_sem.at[at])
        for at, span in enumerate(spans)
    ]
    weight_copies[0].start()
    for copy in token_copies:
        copy.start()
    weight_copies[1].start()

    def ready(at):
        token_copies[at].wait()

    pair_dots(tokens_ref, weight_ref, weight_copies, spans, ready, send_ref, keep_ref, send_hbm, send_sem)


def near_kernel(tokens_ref, weight_hbm, ticket_ref, send_hbm, keep_ref, *scratch):
    weight_ref, send_ref, weight_sem, send_sem = scratch
    narrow_at = lax.axis_index("narrow")
    mine = lax.rem(narrow_at, 2)
    chip = 2 * (narrow_at // 2)
    weight_copies = quarter_copies(weight_hbm, weight_ref, weight_sem, (chip + 1 - mine, chip + mine))
    for copy in weight_copies:
        copy.start()
    spans = row_spans(tokens_ref.shape[0], send_sem.shape[0])
    pair_dots(
        tokens_ref, weight_ref, weight_copies, spans, lambda at: None, send_ref, keep_ref, send_hbm, send_sem
    )


def column_dots(tokens, weight, ticket, columns, far):
    row_total, features = tokens.shape
    hbm = whole_block(pl.ANY)
    blocks = 4
    out_shape = [pltpu.HBM((row_total, columns), F32), VMEM((row_total, columns), F32)]
    scratch = [
        VMEM((2, features, columns), BF16),
        VMEM((row_total, columns), F32),
        pltpu.SemaphoreType.DMA((2,)),
        pltpu.SemaphoreType.DMA((blocks,)),
    ]
    if far:
        out_shape.append(VMEM(tokens.shape, BF16))
        scratch.append(pltpu.SemaphoreType.DMA((blocks,)))
    return pl.pallas_call(
        far_kernel if far else near_kernel,
        out_shape=out_shape,
        in_specs=[hbm if far else whole_block(), hbm, hbm],
        out_specs=[hbm] + [whole_block()] * (len(out_shape) - 1),
        scratch_shapes=scratch,
        compiler_params=pltpu.CompilerParams(vmem_limit_bytes=LIMIT),
        cost_estimate=SMALL if far else LARGE,
        name="far_columns" if far else "near_columns",
    )(in_hbm(tokens) if far else tokens, in_hbm(weight), ticket)


def reload_kernel(tokens_hbm, chosen_ref, ticket_ref, tokens_ref, mask_ref, token_sem):
    copy = pltpu.make_async_copy(tokens_hbm, tokens_ref, token_sem)
    copy.start()
    lanes = 128
    for low in range(0, tokens_ref.shape[0], lanes):
        for at in range(chosen_ref.shape[0]):
            row = chosen_ref[pl.ds(at, 1), pl.ds(low, lanes)]
            column = jnp.broadcast_to(row, (lanes, lanes)).T
            mask_ref[pl.ds(low, lanes), pl.ds(at * lanes, lanes)] = column.astype(BF16)
    copy.wait()


def reload_tokens(tokens, chosen, ticket):
    hbm = whole_block(pl.ANY)
    return pl.pallas_call(
        reload_kernel,
        out_shape=[VMEM(tokens.shape, BF16), VMEM((tokens.shape[0], chosen.shape[0] * 128), BF16)],
        in_specs=[hbm, whole_block(), hbm],
        out_specs=[whole_block()] * 2,
        scratch_shapes=[pltpu.SemaphoreType.DMA],
        compiler_params=pltpu.CompilerParams(vmem_limit_bytes=LIMIT),
        cost_estimate=SMALL,
        name="reload_tokens",
    )(in_hbm(tokens), chosen, ticket)


def base_kernel(keep_ref, arrived_ref, code_ref, out_ref):
    row_total, columns = out_ref.shape
    block = 128
    grades = code_ref[pl.ds(row_total, 16), :].astype(jnp.int32).astype(F32)
    sizes = size_of(grades[:, :block])
    for at in range(row_total // block):
        span = pl.ds(at * block, block)
        size = jnp.broadcast_to(sizes[at : at + 1, :], (block, block)).T
        size = jnp.concatenate([size] * (columns // block), axis=1)
        crossed = code_ref[span, :].astype(jnp.int32).astype(F32) * size
        out_ref[span, :] = keep_ref[span, :] + arrived_ref[span, :] + crossed


def base_rows(keep, arrived, code):
    return pl.pallas_call(
        base_kernel,
        out_shape=VMEM(keep.shape, F32),
        in_specs=[whole_block()] * 3,
        out_specs=whole_block(),
        compiler_params=pltpu.CompilerParams(vmem_limit_bytes=LIMIT),
        cost_estimate=SMALL,
        name="base_rows",
    )(keep, arrived, code)


def shrink_kernel(tokens_ref, chosen_ref, *refs):
    messages, out_ref, stacked = refs[:-2], refs[-2], refs[-1]
    rows, row_total = out_ref.shape
    features = tokens_ref.shape[1]
    block = 256
    for at, message in enumerate(messages):
        stacked[pl.ds(at * rows, rows), :] = message[:, :features]
    for low in range(0, row_total, block):
        span = pl.ds(low, block)
        sums = lax.dot_general(
            tokens_ref[span, :], stacked[...], (((1,), (1,)), ((), ())), preferred_element_type=F32
        ).T
        asked = chosen_ref[:, span] > 0
        total = None
        for at in range(len(messages)):
            term = jnp.where(asked[at : at + 1, :], sums[at * rows : (at + 1) * rows, :], 0.0)
            total = term if total is None else total + term
        out_ref[:, span] = total


def shrink(tokens, chosen, messages):
    row_total, features = tokens.shape
    count = len(messages)
    rows = messages[0].shape[0]
    return pl.pallas_call(
        shrink_kernel,
        out_shape=jax.ShapeDtypeStruct((rows, row_total), F32),
        in_specs=[whole_block()] * (2 + count),
        out_specs=whole_block(),
        scratch_shapes=[VMEM((count * rows, features), BF16)],
        compiler_params=pltpu.CompilerParams(vmem_limit_bytes=LIMIT),
        cost_estimate=SMALL,
        name="shrink",
    )(tokens, chosen, *messages)


def shrunk_code_kernel(keep_ref, arrived_ref, total_ref, code_ref):
    rows, row_total = keep_ref.shape
    total = keep_ref[...] + arrived_ref[...]
    total_ref[...] = total
    grade = grade_of(jnp.max(jnp.abs(total), axis=0, keepdims=True))
    code_ref[pl.ds(0, rows), :] = coded(total, grade)
    grades = jnp.concatenate([grade, jnp.zeros((15, row_total), F32)], axis=0)
    code_ref[pl.ds(rows, 16), :] = grades.astype(jnp.int32).astype(jnp.int16)


def code_shrunk(keep, arrived):
    rows, row_total = keep.shape
    return pl.pallas_call(
        shrunk_code_kernel,
        out_shape=[
            jax.ShapeDtypeStruct((rows, row_total), F32),
            jax.ShapeDtypeStruct((rows + 16, row_total), jnp.int16),
        ],
        in_specs=[whole_block()] * 2,
        out_specs=[whole_block()] * 2,
        compiler_params=pltpu.CompilerParams(vmem_limit_bytes=LIMIT),
        cost_estimate=SMALL,
        name="code_shrunk",
    )(keep, arrived)


def finish_kernel(crossing, features, length_ref, base_ref, mask_ref, part_ref, *refs):
    if crossing:
        code_ref, *refs = refs
    messages, out_ref, stacked = refs[:-2], refs[-2], refs[-1]
    rows = part_ref.shape[0]
    for at, message in enumerate(messages):
        factor = message[:, features:]
        stacked[pl.ds(2 * at * rows, rows), :] = factor
        stacked[pl.ds((2 * at + 1) * rows, rows), :] = factor
    row_total, columns = out_ref.shape
    block = 256
    position = lax.broadcasted_iota(jnp.int32, (LEN, columns), 0)
    for low in range(0, row_total, block):
        span = pl.ds(low, block)
        shrunk = part_ref[:, span]
        if crossing:
            size = size_of(code_ref[pl.ds(rows, 16), span].astype(jnp.int32).astype(F32)[:1, :])
            shrunk = shrunk + code_ref[pl.ds(0, rows), span].astype(jnp.int32).astype(F32) * size
        high = shrunk.astype(BF16).astype(F32)
        both = jnp.concatenate([high, shrunk - high], axis=0).T.astype(BF16)
        spread = jnp.concatenate([both] * len(messages), axis=1) * mask_ref[span, :]
        total = base_ref[span, :] + jnp.dot(spread, stacked[...], preferred_element_type=F32)
        for prompt in range(block // LEN):
            piece = total[prompt * LEN : (prompt + 1) * LEN, :]
            live = position < length_ref[low // LEN + prompt]
            out_ref[pl.ds(low + prompt * LEN, LEN), :] = jnp.where(live, piece, 0.0).astype(BF16)


def finish(lengths, base, mask, part, code, messages, features):
    row_total, columns = base.shape
    count = len(messages)
    rows = messages[0].shape[0]
    operands = [base, mask, part, *code, *messages]
    return pl.pallas_call(
        functools.partial(finish_kernel, bool(code), features),
        out_shape=jax.ShapeDtypeStruct((row_total, columns), BF16),
        in_specs=[whole_block(pltpu.SMEM)] + [whole_block()] * len(operands),
        out_specs=whole_block(),
        scratch_shapes=[VMEM((2 * count * rows, columns), BF16)],
        compiler_params=pltpu.CompilerParams(vmem_limit_bytes=LIMIT),
        cost_estimate=SMALL,
        name="finish",
    )(lengths, *operands)


def on_device(
    tokens,
    value_weight,
    adapter_down_factors,
    adapter_up_factors,
    adapter_choice_index,
    adapter_mask,
    prompt_token_length,
):
    wide_count = lax.axis_size("wide")
    narrow_count = lax.axis_size("narrow")
    wide_at = lax.axis_index("wide")
    owner_portion = adapter_down_factors.shape[0]
    row_total, features = tokens.shape
    per_device = row_total // LEN
    columns = adapter_up_factors.shape[2]

    paired = narrow_count == 4
    sent, ticket = pack_messages(
        adapter_choice_index.reshape(1, -1),
        adapter_mask.reshape(1, -1),
        jnp.swapaxes(adapter_down_factors, 1, 2),
        adapter_up_factors,
        wide_count,
        per_device,
    )
    held = [[sent[0][chunk]] for chunk in range(CHUNKS)]
    for chunk in range(CHUNKS):
        for shift in range(1, wide_count):
            ring = [(at, (at + shift) % wide_count) for at in range(wide_count)]
            held[chunk].append(lax.ppermute(sent[shift][chunk], "wide", ring))

    my_choice = lax.dynamic_slice_in_dim(adapter_choice_index, wide_at * per_device, per_device)
    my_mask = lax.dynamic_slice_in_dim(adapter_mask, wide_at * per_device, per_device)
    my_lengths = lax.dynamic_slice_in_dim(prompt_token_length, wide_at * per_device, per_device)
    owners = (wide_at - jnp.arange(wide_count, dtype=jnp.int32) + wide_count) % wide_count
    local = my_choice[None, :] - owners[:, None] * owner_portion
    matches = (my_mask[None, :] == 1) & (local >= 0) & (local < owner_portion)
    order = jnp.arange(per_device, dtype=jnp.int32)[None, :]
    first = jnp.min(
        jnp.where(matches, order * owner_portion + local, per_device * owner_portion), axis=1
    )
    granted = first % owner_portion
    chosen_prompt = (matches & (local == granted[:, None])).astype(F32)
    chosen = jnp.repeat(chosen_prompt, LEN, axis=1)

    if paired:
        core = [(at, at ^ 1) for at in range(4)]
        across = [(at, at ^ 2) for at in range(4)]
        ticket = lax.ppermute(ticket, "narrow", core)
        far_send, far_keep, held_tokens = column_dots(tokens, value_weight, ticket, columns, True)
        code = code_rows(far_keep, lax.ppermute(far_send, "narrow", core))
        near_send, near_keep = column_dots(held_tokens, value_weight, far_keep, columns, False)
        resident, mask = reload_tokens(tokens, chosen, near_keep)
        base = base_rows(
            near_keep, lax.ppermute(near_send, "narrow", core), lax.ppermute(code, "narrow", across)
        )
        part = shrink(resident, chosen, held[0])
        part, shrunk_code = code_shrunk(part, lax.ppermute(part, "narrow", core))
        crossed = [lax.ppermute(shrunk_code, "narrow", across)]
    else:
        partial_value = jnp.dot(tokens, value_weight, preferred_element_type=F32)
        base = lax.psum_scatter(partial_value, "narrow", scatter_dimension=1, tiled=True)
        resident, mask = reload_tokens(tokens, chosen, ticket)
        part = lax.psum(shrink(resident, chosen, held[0]), "narrow")
        crossed = []
    return finish(my_lengths, base, mask, part, crossed, held[0], features)


def solution(mesh):
    placed = (
        P(("groups", "wide"), "narrow"),
        P("narrow", None),
        P(("groups", "wide"), "narrow", None),
        P(("groups", "wide"), None, "narrow"),
        P("groups"),
        P("groups"),
        P("groups"),
    )
    return jax.shard_map(
        on_device,
        mesh=mesh,
        in_specs=placed,
        out_specs=P(("groups", "wide"), "narrow"),
        check_vma=False,
    )
```

```python
import functools
import math

import jax
import jax.numpy as jnp
from jax import lax
from jax.experimental import pallas as pl
from jax.experimental.pallas import tpu as pltpu
from jax.sharding import PartitionSpec as P

LEN = 32
CHUNKS = 1
LIMIT = 24 * 2**20
VMEM = pltpu.VMEM
F32 = jnp.float32
BF16 = jnp.bfloat16
STEPS = 32767.0
GRADES = 128.0
SMALL = pl.CostEstimate(flops=1, bytes_accessed=1, transcendentals=0)
LARGE = pl.CostEstimate(flops=10**10, bytes_accessed=1, transcendentals=0)


def whole_block(array_memory=VMEM):
    return pl.BlockSpec(memory_space=array_memory)


def in_vmem(array):
    return pltpu.with_memory_space_constraint(array, VMEM)


def in_hbm(array):
    return pltpu.with_memory_space_constraint(array, pltpu.HBM)


def quarter_copies(weight_hbm, weight_ref, weight_sem, quarters):
    columns = weight_ref.shape[2]
    return [
        pltpu.make_async_copy(
            weight_hbm.at[:, pl.ds(pl.multiple_of(quarter * columns, columns), columns)],
            weight_ref.at[at],
            weight_sem.at[at],
        )
        for at, quarter in enumerate(quarters)
    ]


def pack_kernel(wide_count, per_device, *refs):
    message_count = wide_count * CHUNKS
    loads_in, refs = refs[:4], refs[4:]
    messages, refs = refs[:message_count], refs[message_count:]
    ticket_ref, refs = refs[0], refs[1:]
    ticket_ref[...] = jnp.zeros_like(ticket_ref)
    choice_ref, mask_ref, down_ref, up_ref, load_sem, message_sem = refs[:6]
    owner_portion, rank, features = down_ref.shape
    columns = up_ref.shape[2]
    rows = rank // CHUNKS
    loads = [
        pltpu.make_async_copy(source, target, load_sem.at[at])
        for at, (source, target) in enumerate(zip(loads_in, refs[:4]))
    ]
    for copy in loads:
        copy.start()
    loads[0].wait()
    loads[1].wait()
    me = lax.axis_index("wide")
    choice = choice_ref[...]
    prompt = lax.broadcasted_iota(jnp.int32, choice.shape, 1)
    local = choice - me * owner_portion
    wanted = (mask_ref[...] == 1) & (local >= 0) & (local < owner_portion)
    top = jnp.float32(2.0**24)
    key = jnp.where(wanted, (prompt * owner_portion + local).astype(F32), top)
    copies = []
    for shift in range(wide_count):
        reader = lax.rem(me + shift, wide_count)
        low = reader * per_device
        inside = (prompt >= low) & (prompt < low + per_device)
        first = jnp.min(jnp.where(inside, key, top))
        found = jnp.where(first < top, first, 0.0).astype(jnp.int32)
        adapter = lax.rem(found, owner_portion)
        for chunk in range(CHUNKS):
            at = shift * CHUNKS + chunk
            out = messages[at]
            span = pl.ds(chunk * rows, rows)
            copies.append(
                pltpu.make_async_copy(
                    down_ref.at[adapter, span, :], out.at[:, pl.ds(0, features)], message_sem.at[2 * at]
                )
            )
            copies.append(
                pltpu.make_async_copy(
                    up_ref.at[adapter, span, :],
                    out.at[:, pl.ds(features, columns)],
                    message_sem.at[2 * at + 1],
                )
            )
    loads[2].wait()
    loads[3].wait()
    for copy in copies:
        copy.start()
    for copy in copies:
        copy.wait()


def pack_messages(choice, mask, down, up, wide_count, per_device):
    rank, features = down.shape[1:]
    columns = up.shape[2]
    count = wide_count * CHUNKS
    hbm = whole_block(pl.ANY)
    operands = [choice, mask, down, up]
    scratch = [VMEM(operand.shape, operand.dtype) for operand in operands]
    scratch += [pltpu.SemaphoreType.DMA((4,)), pltpu.SemaphoreType.DMA((2 * count,))]
    out_shape = [pltpu.HBM((rank // CHUNKS, features + columns), BF16)] * count
    out_specs = [hbm] * count + [whole_block()]
    out_shape += [jax.ShapeDtypeStruct((8, 128), F32)]
    out = pl.pallas_call(
        functools.partial(pack_kernel, wide_count, per_device),
        out_shape=out_shape,
        in_specs=[hbm] * len(operands),
        out_specs=out_specs,
        scratch_shapes=scratch,
        compiler_params=pltpu.CompilerParams(vmem_limit_bytes=LIMIT),
        cost_estimate=SMALL,
        name="pack_messages",
    )(*[in_hbm(operand) for operand in operands])
    return [out[shift * CHUNKS : (shift + 1) * CHUNKS] for shift in range(wide_count)], out[-1]


def grade_of(size):
    return jnp.ceil(jnp.log(jnp.maximum(size, 2.0**-120)) * (GRADES / math.log(2.0)))


def size_of(grade):
    return jnp.exp2(grade * (1.0 / GRADES)) * (1.0 / STEPS)


def coded(total, grade):
    scaled = total * jnp.exp2(grade * (-1.0 / GRADES)) * STEPS
    return jnp.clip(jnp.round(scaled), -STEPS, STEPS).astype(jnp.int32).astype(jnp.int16)


def code_kernel(keep_ref, arrived_ref, code_ref):
    block = 128
    row_total, columns = keep_ref.shape
    grades = []
    for at in range(row_total // block):
        span = pl.ds(at * block, block)
        total = keep_ref[span, :] + arrived_ref[span, :]
        grade = grade_of(jnp.max(jnp.abs(total), axis=1, keepdims=True))
        code_ref[span, :] = coded(total, grade)
        grades.append(jnp.broadcast_to(grade, (block, block)).T[:1, :])
    grades = jnp.concatenate(grades + [jnp.zeros((16 - len(grades), block), F32)], axis=0)
    grades = jnp.concatenate([grades, jnp.zeros((16, columns - block), F32)], axis=1)
    code_ref[pl.ds(row_total, 16), :] = grades.astype(jnp.int32).astype(jnp.int16)


def code_rows(keep, arrived):
    row_total, columns = keep.shape
    return pl.pallas_call(
        code_kernel,
        out_shape=VMEM((row_total + 16, columns), jnp.int16),
        in_specs=[whole_block()] * 2,
        out_specs=whole_block(),
        compiler_params=pltpu.CompilerParams(vmem_limit_bytes=LIMIT),
        cost_estimate=SMALL,
        name="code_rows",
    )(keep, arrived)


def pair_dots(tokens_ref, weight_ref, weight_copies, send_ref, keep_ref, send_hbm, send_sem):
    block = 256
    spans = [pl.ds(low, block) for low in range(0, tokens_ref.shape[0], block)]
    for span in spans:
        send_ref[span, :] = jnp.dot(tokens_ref[span, :], weight_ref[0], preferred_element_type=F32)
    copy = pltpu.make_async_copy(send_ref, send_hbm, send_sem)
    copy.start()
    weight_copies[1].wait()
    for span in spans:
        keep_ref[span, :] = jnp.dot(tokens_ref[span, :], weight_ref[1], preferred_element_type=F32)
    copy.wait()


def far_kernel(tokens_hbm, weight_hbm, ticket_ref, send_hbm, keep_ref, tokens_ref, *scratch):
    weight_ref, send_ref, weight_sem, send_sem, token_sem = scratch
    narrow_at = lax.axis_index("narrow")
    mine = lax.rem(narrow_at, 2)
    chip = 2 * ((narrow_at // 2) ^ 1)
    weight_copies = quarter_copies(weight_hbm, weight_ref, weight_sem, (chip + 1 - mine, chip + mine))
    token_copy = pltpu.make_async_copy(tokens_hbm, tokens_ref, token_sem)
    weight_copies[0].start()
    token_copy.start()
    weight_copies[1].start()
    weight_copies[0].wait()
    token_copy.wait()
    pair_dots(tokens_ref, weight_ref, weight_copies, send_ref, keep_ref, send_hbm, send_sem)


def near_kernel(tokens_ref, weight_hbm, ticket_ref, send_hbm, keep_ref, *scratch):
    weight_ref, send_ref, weight_sem, send_sem = scratch
    narrow_at = lax.axis_index("narrow")
    mine = lax.rem(narrow_at, 2)
    chip = 2 * (narrow_at // 2)
    weight_copies = quarter_copies(weight_hbm, weight_ref, weight_sem, (chip + 1 - mine, chip + mine))
    for copy in weight_copies:
        copy.start()
    weight_copies[0].wait()
    pair_dots(tokens_ref, weight_ref, weight_copies, send_ref, keep_ref, send_hbm, send_sem)


def column_dots(tokens, weight, ticket, columns, far):
    row_total, features = tokens.shape
    hbm = whole_block(pl.ANY)
    out_shape = [pltpu.HBM((row_total, columns), F32), VMEM((row_total, columns), F32)]
    scratch = [
        VMEM((2, features, columns), BF16),
        VMEM((row_total, columns), F32),
        pltpu.SemaphoreType.DMA((2,)),
        pltpu.SemaphoreType.DMA,
    ]
    if far:
        out_shape.append(VMEM(tokens.shape, BF16))
        scratch.append(pltpu.SemaphoreType.DMA)
    return pl.pallas_call(
        far_kernel if far else near_kernel,
        out_shape=out_shape,
        in_specs=[hbm if far else whole_block(), hbm, hbm],
        out_specs=[hbm] + [whole_block()] * (len(out_shape) - 1),
        scratch_shapes=scratch,
        compiler_params=pltpu.CompilerParams(vmem_limit_bytes=LIMIT),
        cost_estimate=SMALL if far else LARGE,
        name="far_columns" if far else "near_columns",
    )(in_hbm(tokens) if far else tokens, in_hbm(weight), ticket)


def reload_kernel(tokens_hbm, chosen_ref, ticket_ref, tokens_ref, mask_ref, token_sem):
    copy = pltpu.make_async_copy(tokens_hbm, tokens_ref, token_sem)
    copy.start()
    lanes = 128
    for low in range(0, tokens_ref.shape[0], lanes):
        for at in range(chosen_ref.shape[0]):
            row = chosen_ref[pl.ds(at, 1), pl.ds(low, lanes)]
            column = jnp.broadcast_to(row, (lanes, lanes)).T
            mask_ref[pl.ds(low, lanes), pl.ds(at * lanes, lanes)] = column.astype(BF16)
    copy.wait()


def reload_tokens(tokens, chosen, ticket):
    hbm = whole_block(pl.ANY)
    return pl.pallas_call(
        reload_kernel,
        out_shape=[VMEM(tokens.shape, BF16), VMEM((tokens.shape[0], chosen.shape[0] * 128), BF16)],
        in_specs=[hbm, whole_block(), hbm],
        out_specs=[whole_block()] * 2,
        scratch_shapes=[pltpu.SemaphoreType.DMA],
        compiler_params=pltpu.CompilerParams(vmem_limit_bytes=LIMIT),
        cost_estimate=SMALL,
        name="reload_tokens",
    )(in_hbm(tokens), chosen, ticket)


def base_kernel(length_ref, keep_ref, arrived_ref, code_ref, out_ref):
    row_total, columns = out_ref.shape
    block = 128
    position = lax.broadcasted_iota(jnp.int32, (LEN, columns), 0)
    grades = code_ref[pl.ds(row_total, 16), :].astype(jnp.int32).astype(F32)
    sizes = size_of(grades[:, :block])
    for at in range(row_total // block):
        span = pl.ds(at * block, block)
        size = jnp.broadcast_to(sizes[at : at + 1, :], (block, block)).T
        size = jnp.concatenate([size] * (columns // block), axis=1)
        crossed = code_ref[span, :].astype(jnp.int32).astype(F32) * size
        total = keep_ref[span, :] + arrived_ref[span, :] + crossed
        for prompt in range(block // LEN):
            low = at * block + prompt * LEN
            live = position < length_ref[low // LEN]
            piece = total[prompt * LEN : (prompt + 1) * LEN, :]
            out_ref[pl.ds(low, LEN), :] = jnp.where(live, piece, 0.0)


def base_rows(lengths, keep, arrived, code):
    return pl.pallas_call(
        base_kernel,
        out_shape=VMEM(keep.shape, F32),
        in_specs=[whole_block(pltpu.SMEM)] + [whole_block()] * 3,
        out_specs=whole_block(),
        compiler_params=pltpu.CompilerParams(vmem_limit_bytes=LIMIT),
        cost_estimate=SMALL,
        name="base_rows",
    )(lengths, keep, arrived, code)


def shrink_kernel(start, stacking, tokens_ref, chosen_ref, *refs):
    if stacking:
        messages, (out_ref, stacked) = refs[:-2], refs[-2:]
    else:
        stacked, out_ref = refs
    rows, row_total = out_ref.shape
    features = tokens_ref.shape[1]
    count = stacked.shape[0] // rows
    block = 256
    if stacking:
        for at, message in enumerate(messages):
            stacked[pl.ds(at * rows, rows), :] = message[:, :features]
    for low in range(0, row_total, block):
        span = pl.ds(start + low, block)
        sums = lax.dot_general(
            tokens_ref[span, :], stacked[...], (((1,), (1,)), ((), ())), preferred_element_type=F32
        ).T
        asked = chosen_ref[:, span] > 0
        total = None
        for at in range(count):
            term = jnp.where(asked[at : at + 1, :], sums[at * rows : (at + 1) * rows, :], 0.0)
            total = term if total is None else total + term
        out_ref[:, pl.ds(low, block)] = total


def shrink(tokens, chosen, factors, rows, start, row_total):
    features = tokens.shape[1]
    stacking = start == 0
    out_shape = [jax.ShapeDtypeStruct((rows, row_total), F32)]
    if stacking:
        out_shape.append(VMEM((len(factors) * rows, features), BF16))
    return pl.pallas_call(
        functools.partial(shrink_kernel, start, stacking),
        out_shape=out_shape,
        in_specs=[whole_block()] * (2 + len(factors)),
        out_specs=[whole_block()] * len(out_shape),
        compiler_params=pltpu.CompilerParams(vmem_limit_bytes=LIMIT),
        cost_estimate=SMALL,
        name="shrink",
    )(tokens, chosen, *factors)


def shrunk_code_kernel(keep_ref, arrived_ref, total_ref, code_ref):
    rows, row_total = keep_ref.shape
    total = keep_ref[...] + arrived_ref[...]
    total_ref[...] = total
    grade = grade_of(jnp.max(jnp.abs(total), axis=0, keepdims=True))
    code_ref[pl.ds(0, rows), :] = coded(total, grade)
    grades = jnp.concatenate([grade, jnp.zeros((15, row_total), F32)], axis=0)
    code_ref[pl.ds(rows, 16), :] = grades.astype(jnp.int32).astype(jnp.int16)


def code_shrunk(keep, arrived):
    rows, row_total = keep.shape
    return pl.pallas_call(
        shrunk_code_kernel,
        out_shape=[
            jax.ShapeDtypeStruct((rows, row_total), F32),
            jax.ShapeDtypeStruct((rows + 16, row_total), jnp.int16),
        ],
        in_specs=[whole_block()] * 2,
        out_specs=[whole_block()] * 2,
        compiler_params=pltpu.CompilerParams(vmem_limit_bytes=LIMIT),
        cost_estimate=SMALL,
        name="code_shrunk",
    )(keep, arrived)


def finish_kernel(start, crossing, features, base_ref, mask_ref, part_ref, *refs):
    if crossing:
        code_ref, *refs = refs
    if start:
        refs = refs[1:]
    messages, (out_hbm, out_ref, stacked, sem) = refs[:-4], refs[-4:]
    rows = part_ref.shape[0]
    for at, message in enumerate(messages):
        factor = message[:, features:]
        stacked[pl.ds(2 * at * rows, rows), :] = factor
        stacked[pl.ds((2 * at + 1) * rows, rows), :] = factor
    row_total, columns = out_ref.shape
    block = 256
    copies = []
    for low in range(0, row_total, block):
        here = pl.ds(low, block)
        span = pl.ds(start + low, block)
        shrunk = part_ref[:, here]
        if crossing:
            size = size_of(code_ref[pl.ds(rows, 16), here].astype(jnp.int32).astype(F32)[:1, :])
            shrunk = shrunk + code_ref[pl.ds(0, rows), here].astype(jnp.int32).astype(F32) * size
        high = shrunk.astype(BF16).astype(F32)
        both = jnp.concatenate([high, shrunk - high], axis=0).T.astype(BF16)
        spread = jnp.concatenate([both] * len(messages), axis=1) * mask_ref[span, :]
        total = base_ref[span, :] + jnp.dot(spread, stacked[...], preferred_element_type=F32)
        out_ref[here, :] = total.astype(BF16)
        copies.append(pltpu.make_async_copy(out_ref.at[here, :], out_hbm.at[span, :], sem.at[low // block]))
        copies[-1].start()
    for copy in copies:
        copy.wait()


def finish(base, mask, part, code, earlier, messages, features, start):
    columns = base.shape[1]
    count = len(messages)
    rows, row_total = part.shape
    operands = [base, mask, part, *code, *earlier, *messages]
    hbm = whole_block(pl.ANY)
    in_specs = [whole_block()] * (3 + len(code))
    aliases = {len(in_specs): 0} if earlier else {}
    in_specs += [hbm] * len(earlier) + [whole_block()] * count
    return pl.pallas_call(
        functools.partial(finish_kernel, start, bool(code), features),
        out_shape=jax.ShapeDtypeStruct(base.shape, BF16),
        in_specs=in_specs,
        out_specs=hbm,
        input_output_aliases=aliases,
        scratch_shapes=[
            VMEM((row_total, columns), BF16),
            VMEM((2 * count * rows, columns), BF16),
            pltpu.SemaphoreType.DMA((row_total // 256,)),
        ],
        compiler_params=pltpu.CompilerParams(vmem_limit_bytes=LIMIT),
        cost_estimate=SMALL,
        name="finish",
    )(*operands)


def on_device(
    tokens,
    value_weight,
    adapter_down_factors,
    adapter_up_factors,
    adapter_choice_index,
    adapter_mask,
    prompt_token_length,
):
    wide_count = lax.axis_size("wide")
    narrow_count = lax.axis_size("narrow")
    wide_at = lax.axis_index("wide")
    owner_portion = adapter_down_factors.shape[0]
    row_total, features = tokens.shape
    per_device = row_total // LEN
    columns = adapter_up_factors.shape[2]

    paired = narrow_count == 4
    sent, ticket = pack_messages(
        adapter_choice_index.reshape(1, -1),
        adapter_mask.reshape(1, -1),
        jnp.swapaxes(adapter_down_factors, 1, 2),
        adapter_up_factors,
        wide_count,
        per_device,
    )
    held = [[sent[0][chunk]] for chunk in range(CHUNKS)]
    for chunk in range(CHUNKS):
        for shift in range(1, wide_count):
            ring = [(at, (at + shift) % wide_count) for at in range(wide_count)]
            held[chunk].append(lax.ppermute(sent[shift][chunk], "wide", ring))

    my_choice = lax.dynamic_slice_in_dim(adapter_choice_index, wide_at * per_device, per_device)
    my_mask = lax.dynamic_slice_in_dim(adapter_mask, wide_at * per_device, per_device)
    my_lengths = lax.dynamic_slice_in_dim(prompt_token_length, wide_at * per_device, per_device)
    owners = (wide_at - jnp.arange(wide_count, dtype=jnp.int32) + wide_count) % wide_count
    local = my_choice[None, :] - owners[:, None] * owner_portion
    matches = (my_mask[None, :] == 1) & (local >= 0) & (local < owner_portion)
    order = jnp.arange(per_device, dtype=jnp.int32)[None, :]
    first = jnp.min(
        jnp.where(matches, order * owner_portion + local, per_device * owner_portion), axis=1
    )
    granted = first % owner_portion
    chosen_prompt = (matches & (local == granted[:, None])).astype(F32)
    inside = jnp.arange(LEN, dtype=jnp.int32)[None, :] < my_lengths[:, None]
    chosen = jnp.where(inside[None], chosen_prompt[:, :, None], 0.0).reshape(wide_count, row_total)

    if paired:
        core = [(at, at ^ 1) for at in range(4)]
        across = [(at, at ^ 2) for at in range(4)]
        ticket = lax.ppermute(ticket, "narrow", core)
        far_send, far_keep, held_tokens = column_dots(tokens, value_weight, ticket, columns, True)
        far_arrived = lax.ppermute(far_send, "narrow", core)
        code = code_rows(in_vmem(far_keep), in_vmem(far_arrived))
        near_send, near_keep = column_dots(held_tokens, value_weight, far_keep, columns, False)
        resident, mask = reload_tokens(tokens, chosen, near_keep)
        base = base_rows(
            my_lengths,
            near_keep,
            lax.ppermute(near_send, "narrow", core),
            lax.ppermute(code, "narrow", across),
        )
        pieces = 2
    else:
        partial_value = jnp.dot(tokens, value_weight, preferred_element_type=F32)
        base = lax.psum_scatter(partial_value, "narrow", scatter_dimension=1, tiled=True)
        base = jnp.where(inside.reshape(row_total, 1), base, 0.0)
        resident, mask = reload_tokens(tokens, chosen, ticket)
        pieces = 1
    rows = adapter_down_factors.shape[2]
    piece = row_total // pieces
    factors, values = held[0], []
    for start in range(0, row_total, piece):
        part, *stacked = shrink(resident, chosen, factors, rows, start, piece)
        factors = stacked or factors
        crossed = []
        if paired:
            part, shrunk_code = code_shrunk(part, lax.ppermute(part, "narrow", core))
            crossed = [lax.ppermute(shrunk_code, "narrow", across)]
        else:
            part = lax.psum(part, "narrow")
        values = [finish(base, mask, part, crossed, values, held[0], features, start)]
    return values[0]


def solution(mesh):
    placed = (
        P(("groups", "wide"), "narrow"),
        P("narrow", None),
        P(("groups", "wide"), "narrow", None),
        P(("groups", "wide"), None, "narrow"),
        P("groups"),
        P("groups"),
        P("groups"),
    )
    return jax.shard_map(
        on_device,
        mesh=mesh,
        in_specs=placed,
        out_specs=P(("groups", "wide"), "narrow"),
        check_vma=False,
    )
```

```python
import functools
import math

import jax
import jax.numpy as jnp
from jax import lax
from jax.experimental import pallas as pl
from jax.experimental.pallas import tpu as pltpu
from jax.sharding import PartitionSpec as P

LEN = 32
CHUNKS = 1
LIMIT = 24 * 2**20
VMEM = pltpu.VMEM
F32 = jnp.float32
BF16 = jnp.bfloat16
STEPS = 32767.0
GRADES = 128.0
SMALL = pl.CostEstimate(flops=1, bytes_accessed=1, transcendentals=0)
LARGE = pl.CostEstimate(flops=10**10, bytes_accessed=1, transcendentals=0)


def whole_block(array_memory=VMEM):
    return pl.BlockSpec(memory_space=array_memory)


def in_vmem(array):
    return pltpu.with_memory_space_constraint(array, VMEM)


def in_hbm(array):
    return pltpu.with_memory_space_constraint(array, pltpu.HBM)


def quarter_copies(weight_hbm, weight_ref, weight_sem, quarters):
    columns = weight_ref.shape[2]
    return [
        pltpu.make_async_copy(
            weight_hbm.at[:, pl.ds(pl.multiple_of(quarter * columns, columns), columns)],
            weight_ref.at[at],
            weight_sem.at[at],
        )
        for at, quarter in enumerate(quarters)
    ]


def pack_kernel(wide_count, per_device, *refs):
    message_count = wide_count * CHUNKS
    loads_in, refs = refs[:5], refs[5:]
    messages, refs = refs[:message_count], refs[message_count:]
    ticket_ref, settings_ref, *refs = refs
    ticket_ref[...] = jnp.zeros_like(ticket_ref)
    choice_ref, mask_ref, down_ref, up_ref, length_ref, load_sem, message_sem = refs
    owner_portion, rank, features = down_ref.shape
    columns = up_ref.shape[2]
    rows = rank // CHUNKS
    loads = [
        pltpu.make_async_copy(source, target, load_sem.at[at])
        for at, (source, target) in enumerate(zip(loads_in, refs[:5]))
    ]
    for copy in loads:
        copy.start()
    loads[0].wait()
    loads[1].wait()
    me = lax.axis_index("wide")
    choice = choice_ref[...]
    prompt = lax.broadcasted_iota(jnp.int32, choice.shape, 1)
    local = choice - me * owner_portion
    wanted = (mask_ref[...] == 1) & (local >= 0) & (local < owner_portion)
    top = jnp.float32(2.0**24)
    key = jnp.where(wanted, (prompt * owner_portion + local).astype(F32), top)
    copies = []
    for shift in range(wide_count):
        reader = lax.rem(me + shift, wide_count)
        low = reader * per_device
        inside = (prompt >= low) & (prompt < low + per_device)
        first = jnp.min(jnp.where(inside, key, top))
        found = jnp.where(first < top, first, 0.0).astype(jnp.int32)
        adapter = lax.rem(found, owner_portion)
        for chunk in range(CHUNKS):
            at = shift * CHUNKS + chunk
            out = messages[at]
            span = pl.ds(chunk * rows, rows)
            copies.append(
                pltpu.make_async_copy(
                    down_ref.at[adapter, span, :], out.at[:, pl.ds(0, features)], message_sem.at[2 * at]
                )
            )
            copies.append(
                pltpu.make_async_copy(
                    up_ref.at[adapter, span, :],
                    out.at[:, pl.ds(features, columns)],
                    message_sem.at[2 * at + 1],
                )
            )
    loads[2].wait()
    loads[3].wait()
    for copy in copies:
        copy.start()
    loads[4].wait()
    for at, source in enumerate((choice_ref, mask_ref, length_ref)):
        settings_ref[pl.ds(at, 1), :] = source[...]
    for copy in copies:
        copy.wait()


def pack_messages(choice, mask, lengths, down, up, wide_count, per_device):
    rank, features = down.shape[1:]
    columns = up.shape[2]
    count = wide_count * CHUNKS
    hbm = whole_block(pl.ANY)
    operands = [choice, mask, down, up, lengths]
    scratch = [VMEM(operand.shape, operand.dtype) for operand in operands]
    scratch += [pltpu.SemaphoreType.DMA((5,)), pltpu.SemaphoreType.DMA((2 * count,))]
    out_shape = [pltpu.HBM((rank // CHUNKS, features + columns), BF16)] * count
    out_specs = [hbm] * count + [whole_block()] * 2
    out_shape += [jax.ShapeDtypeStruct((8, 128), F32), jax.ShapeDtypeStruct((3, choice.shape[1]), jnp.int32)]
    out = pl.pallas_call(
        functools.partial(pack_kernel, wide_count, per_device),
        out_shape=out_shape,
        in_specs=[hbm] * len(operands),
        out_specs=out_specs,
        scratch_shapes=scratch,
        compiler_params=pltpu.CompilerParams(vmem_limit_bytes=LIMIT),
        cost_estimate=SMALL,
        name="pack_messages",
    )(*[in_hbm(operand) for operand in operands])
    return [out[shift * CHUNKS : (shift + 1) * CHUNKS] for shift in range(wide_count)], *out[count:]


def grade_of(size):
    return jnp.ceil(jnp.log(jnp.maximum(size, 2.0**-120)) * (GRADES / math.log(2.0)))


def size_of(grade):
    return jnp.exp2(grade * (1.0 / GRADES)) * (1.0 / STEPS)


def coded(total, grade):
    scaled = total * jnp.exp2(grade * (-1.0 / GRADES)) * STEPS
    return jnp.clip(jnp.round(scaled), -STEPS, STEPS).astype(jnp.int32).astype(jnp.int16)


def code_kernel(keep_ref, arrived_ref, code_ref):
    block = 128
    row_total, columns = keep_ref.shape
    grades = []
    for at in range(row_total // block):
        span = pl.ds(at * block, block)
        total = keep_ref[span, :] + arrived_ref[span, :]
        grade = grade_of(jnp.max(jnp.abs(total), axis=1, keepdims=True))
        code_ref[span, :] = coded(total, grade)
        grades.append(jnp.broadcast_to(grade, (block, block)).T[:1, :])
    grades = jnp.concatenate(grades + [jnp.zeros((16 - len(grades), block), F32)], axis=0)
    grades = jnp.concatenate([grades, jnp.zeros((16, columns - block), F32)], axis=1)
    code_ref[pl.ds(row_total, 16), :] = grades.astype(jnp.int32).astype(jnp.int16)


def code_rows(keep, arrived):
    row_total, columns = keep.shape
    return pl.pallas_call(
        code_kernel,
        out_shape=VMEM((row_total + 16, columns), jnp.int16),
        in_specs=[whole_block()] * 2,
        out_specs=whole_block(),
        compiler_params=pltpu.CompilerParams(vmem_limit_bytes=LIMIT),
        cost_estimate=SMALL,
        name="code_rows",
    )(keep, arrived)


def pair_dots(tokens_ref, weight_ref, weight_copies, send_ref, keep_ref, send_hbm, send_sem):
    block = 256
    spans = [pl.ds(low, block) for low in range(0, tokens_ref.shape[0], block)]
    for span in spans:
        send_ref[span, :] = jnp.dot(tokens_ref[span, :], weight_ref[0], preferred_element_type=F32)
    copy = pltpu.make_async_copy(send_ref, send_hbm, send_sem)
    copy.start()
    weight_copies[1].wait()
    for span in spans:
        keep_ref[span, :] = jnp.dot(tokens_ref[span, :], weight_ref[1], preferred_element_type=F32)
    copy.wait()


def far_kernel(tokens_hbm, weight_hbm, ticket_ref, send_hbm, keep_ref, tokens_ref, *scratch):
    weight_ref, send_ref, weight_sem, send_sem, token_sem = scratch
    narrow_at = lax.axis_index("narrow")
    mine = lax.rem(narrow_at, 2)
    chip = 2 * ((narrow_at // 2) ^ 1)
    weight_copies = quarter_copies(weight_hbm, weight_ref, weight_sem, (chip + 1 - mine, chip + mine))
    token_copy = pltpu.make_async_copy(tokens_hbm, tokens_ref, token_sem)
    weight_copies[0].start()
    token_copy.start()
    weight_copies[1].start()
    weight_copies[0].wait()
    token_copy.wait()
    pair_dots(tokens_ref, weight_ref, weight_copies, send_ref, keep_ref, send_hbm, send_sem)


def near_kernel(tokens_ref, weight_hbm, ticket_ref, send_hbm, keep_ref, *scratch):
    weight_ref, send_ref, weight_sem, send_sem = scratch
    narrow_at = lax.axis_index("narrow")
    mine = lax.rem(narrow_at, 2)
    chip = 2 * (narrow_at // 2)
    weight_copies = quarter_copies(weight_hbm, weight_ref, weight_sem, (chip + 1 - mine, chip + mine))
    for copy in weight_copies:
        copy.start()
    weight_copies[0].wait()
    pair_dots(tokens_ref, weight_ref, weight_copies, send_ref, keep_ref, send_hbm, send_sem)


def column_dots(tokens, weight, ticket, columns, far):
    row_total, features = tokens.shape
    hbm = whole_block(pl.ANY)
    out_shape = [pltpu.HBM((row_total, columns), F32), VMEM((row_total, columns), F32)]
    scratch = [
        VMEM((2, features, columns), BF16),
        VMEM((row_total, columns), F32),
        pltpu.SemaphoreType.DMA((2,)),
        pltpu.SemaphoreType.DMA,
    ]
    if far:
        out_shape.append(VMEM(tokens.shape, BF16))
        scratch.append(pltpu.SemaphoreType.DMA)
    return pl.pallas_call(
        far_kernel if far else near_kernel,
        out_shape=out_shape,
        in_specs=[hbm if far else whole_block(), hbm, hbm],
        out_specs=[hbm] + [whole_block()] * (len(out_shape) - 1),
        scratch_shapes=scratch,
        compiler_params=pltpu.CompilerParams(vmem_limit_bytes=LIMIT),
        cost_estimate=SMALL if far else LARGE,
        name="far_columns" if far else "near_columns",
    )(in_hbm(tokens) if far else tokens, in_hbm(weight), ticket)


def reload_kernel(tokens_hbm, chosen_ref, ticket_ref, tokens_ref, mask_ref, token_sem):
    copy = pltpu.make_async_copy(tokens_hbm, tokens_ref, token_sem)
    copy.start()
    lanes = 128
    for low in range(0, tokens_ref.shape[0], lanes):
        for at in range(chosen_ref.shape[0]):
            row = chosen_ref[pl.ds(at, 1), pl.ds(low, lanes)]
            column = jnp.broadcast_to(row, (lanes, lanes)).T
            mask_ref[pl.ds(low, lanes), pl.ds(at * lanes, lanes)] = column.astype(BF16)
    copy.wait()


def reload_tokens(tokens, chosen, ticket):
    hbm = whole_block(pl.ANY)
    return pl.pallas_call(
        reload_kernel,
        out_shape=[VMEM(tokens.shape, BF16), VMEM((tokens.shape[0], chosen.shape[0] * 128), BF16)],
        in_specs=[hbm, whole_block(), hbm],
        out_specs=[whole_block()] * 2,
        scratch_shapes=[pltpu.SemaphoreType.DMA],
        compiler_params=pltpu.CompilerParams(vmem_limit_bytes=LIMIT),
        cost_estimate=SMALL,
        name="reload_tokens",
    )(in_hbm(tokens), chosen, ticket)


def base_kernel(length_ref, keep_ref, arrived_ref, code_ref, out_ref):
    row_total, columns = out_ref.shape
    block = 128
    position = lax.broadcasted_iota(jnp.int32, (LEN, columns), 0)
    grades = code_ref[pl.ds(row_total, 16), :].astype(jnp.int32).astype(F32)
    sizes = size_of(grades[:, :block])
    for at in range(row_total // block):
        span = pl.ds(at * block, block)
        size = jnp.broadcast_to(sizes[at : at + 1, :], (block, block)).T
        size = jnp.concatenate([size] * (columns // block), axis=1)
        crossed = code_ref[span, :].astype(jnp.int32).astype(F32) * size
        total = keep_ref[span, :] + arrived_ref[span, :] + crossed
        for prompt in range(block // LEN):
            low = at * block + prompt * LEN
            live = position < length_ref[low // LEN]
            piece = total[prompt * LEN : (prompt + 1) * LEN, :]
            out_ref[pl.ds(low, LEN), :] = jnp.where(live, piece, 0.0)


def base_rows(lengths, keep, arrived, code):
    return pl.pallas_call(
        base_kernel,
        out_shape=VMEM(keep.shape, F32),
        in_specs=[whole_block(pltpu.SMEM)] + [whole_block()] * 3,
        out_specs=whole_block(),
        compiler_params=pltpu.CompilerParams(vmem_limit_bytes=LIMIT),
        cost_estimate=SMALL,
        name="base_rows",
    )(lengths, keep, arrived, code)


def piece_start(kind, length):
    if kind == 0:
        return 0
    mine = lax.rem(lax.axis_index("narrow"), 2)
    return pl.multiple_of((mine if kind == 1 else 1 - mine) * length, length)


def shrink_kernel(kind, stacking, tokens_ref, chosen_ref, *refs):
    if stacking:
        messages, (out_ref, stacked) = refs[:-2], refs[-2:]
    else:
        stacked, out_ref = refs
    rows, row_total = out_ref.shape
    features = tokens_ref.shape[1]
    count = stacked.shape[0] // rows
    block = 256
    start = piece_start(kind, row_total)
    if stacking:
        for at, message in enumerate(messages):
            stacked[pl.ds(at * rows, rows), :] = message[:, :features]
    for low in range(0, row_total, block):
        span = pl.ds(pl.multiple_of(start + low, block), block)
        sums = lax.dot_general(
            tokens_ref[span, :], stacked[...], (((1,), (1,)), ((), ())), preferred_element_type=F32
        ).T
        asked = chosen_ref[:, span] > 0
        total = None
        for at in range(count):
            term = jnp.where(asked[at : at + 1, :], sums[at * rows : (at + 1) * rows, :], 0.0)
            total = term if total is None else total + term
        out_ref[:, pl.ds(low, block)] = total


def shrink(tokens, chosen, factors, rows, kind, row_total):
    features = tokens.shape[1]
    stacking = len(factors) > 1
    out_shape = [jax.ShapeDtypeStruct((rows, row_total), F32)]
    if stacking:
        out_shape.append(VMEM((len(factors) * rows, features), BF16))
    return pl.pallas_call(
        functools.partial(shrink_kernel, kind, stacking),
        out_shape=out_shape,
        in_specs=[whole_block()] * (2 + len(factors)),
        out_specs=[whole_block()] * len(out_shape),
        compiler_params=pltpu.CompilerParams(vmem_limit_bytes=LIMIT),
        cost_estimate=SMALL,
        name="shrink",
    )(tokens, chosen, *factors)


def shrunk_code_kernel(keep_ref, arrived_ref, total_ref, code_ref):
    rows, row_total = keep_ref.shape
    total = keep_ref[...] + arrived_ref[...]
    total_ref[...] = total
    grade = grade_of(jnp.max(jnp.abs(total), axis=0, keepdims=True))
    code_ref[pl.ds(0, rows), :] = coded(total, grade)
    grades = jnp.concatenate([grade, jnp.zeros((15, row_total), F32)], axis=0)
    code_ref[pl.ds(rows, 16), :] = grades.astype(jnp.int32).astype(jnp.int16)


def code_shrunk(keep, arrived):
    rows, row_total = keep.shape
    return pl.pallas_call(
        shrunk_code_kernel,
        out_shape=[
            jax.ShapeDtypeStruct((rows, row_total), F32),
            jax.ShapeDtypeStruct((rows + 16, row_total), jnp.int16),
        ],
        in_specs=[whole_block()] * 2,
        out_specs=[whole_block()] * 2,
        compiler_params=pltpu.CompilerParams(vmem_limit_bytes=LIMIT),
        cost_estimate=SMALL,
        name="code_shrunk",
    )(keep, arrived)


def sum_kernel(total_ref, code_ref, ticket_ref, out_ref):
    rows = total_ref.shape[0]
    size = size_of(code_ref[pl.ds(rows, 16), :].astype(jnp.int32).astype(F32)[:1, :])
    out_ref[...] = total_ref[...] + code_ref[pl.ds(0, rows), :].astype(jnp.int32).astype(F32) * size


def sum_shrunk(total, code, ticket):
    return pl.pallas_call(
        sum_kernel,
        out_shape=jax.ShapeDtypeStruct(total.shape, F32),
        in_specs=[whole_block()] * 2 + [whole_block(pl.ANY)],
        out_specs=whole_block(),
        compiler_params=pltpu.CompilerParams(vmem_limit_bytes=LIMIT),
        cost_estimate=SMALL,
        name="sum_shrunk",
    )(total, code, ticket)


def finish_kernel(kind, features, base_ref, mask_ref, part_ref, *refs):
    if kind == 2:
        refs = refs[1:]
    messages, (out_hbm, out_ref, stacked, sem) = refs[:-4], refs[-4:]
    rows = part_ref.shape[0]
    for at, message in enumerate(messages):
        factor = message[:, features:]
        stacked[pl.ds(2 * at * rows, rows), :] = factor
        stacked[pl.ds((2 * at + 1) * rows, rows), :] = factor
    row_total, columns = out_ref.shape
    block = 256
    start = piece_start(kind, row_total)
    copies = []
    for low in range(0, row_total, block):
        here = pl.ds(low, block)
        span = pl.ds(pl.multiple_of(start + low, block), block)
        shrunk = part_ref[:, here]
        high = shrunk.astype(BF16).astype(F32)
        both = jnp.concatenate([high, shrunk - high], axis=0).T.astype(BF16)
        spread = jnp.concatenate([both] * len(messages), axis=1) * mask_ref[span, :]
        total = base_ref[span, :] + jnp.dot(spread, stacked[...], preferred_element_type=F32)
        out_ref[here, :] = total.astype(BF16)
        copies.append(pltpu.make_async_copy(out_ref.at[here, :], out_hbm.at[span, :], sem.at[low // block]))
        copies[-1].start()
    for copy in copies:
        copy.wait()


def finish(base, mask, part, earlier, messages, features, kind):
    columns = base.shape[1]
    count = len(messages)
    rows, row_total = part.shape
    operands = [base, mask, part, *earlier, *messages]
    hbm = whole_block(pl.ANY)
    in_specs = [whole_block()] * 3
    aliases = {len(in_specs): 0} if earlier else {}
    in_specs += [hbm] * len(earlier) + [whole_block()] * count
    return pl.pallas_call(
        functools.partial(finish_kernel, kind, features),
        out_shape=jax.ShapeDtypeStruct(base.shape, BF16),
        in_specs=in_specs,
        out_specs=hbm,
        input_output_aliases=aliases,
        scratch_shapes=[
            VMEM((row_total, columns), BF16),
            VMEM((2 * count * rows, columns), BF16),
            pltpu.SemaphoreType.DMA((row_total // 256,)),
        ],
        compiler_params=pltpu.CompilerParams(vmem_limit_bytes=LIMIT),
        cost_estimate=SMALL,
        name="finish",
    )(*operands)


def on_device(
    tokens,
    value_weight,
    adapter_down_factors,
    adapter_up_factors,
    adapter_choice_index,
    adapter_mask,
    prompt_token_length,
):
    wide_count = lax.axis_size("wide")
    narrow_count = lax.axis_size("narrow")
    wide_at = lax.axis_index("wide")
    owner_portion = adapter_down_factors.shape[0]
    row_total, features = tokens.shape
    per_device = row_total // LEN
    columns = adapter_up_factors.shape[2]

    paired = narrow_count == 4
    sent, ticket, settings = pack_messages(
        adapter_choice_index.reshape(1, -1),
        adapter_mask.reshape(1, -1),
        prompt_token_length.reshape(1, -1),
        jnp.swapaxes(adapter_down_factors, 1, 2),
        adapter_up_factors,
        wide_count,
        per_device,
    )
    held = [[sent[0][chunk]] for chunk in range(CHUNKS)]
    for chunk in range(CHUNKS):
        for shift in range(1, wide_count):
            ring = [(at, (at + shift) % wide_count) for at in range(wide_count)]
            held[chunk].append(lax.ppermute(sent[shift][chunk], "wide", ring))

    my_settings = lax.dynamic_slice_in_dim(settings, wide_at * per_device, per_device, axis=1)
    my_choice, my_mask, my_lengths = my_settings[0], my_settings[1], my_settings[2]
    owners = (wide_at - jnp.arange(wide_count, dtype=jnp.int32) + wide_count) % wide_count
    local = my_choice[None, :] - owners[:, None] * owner_portion
    matches = (my_mask[None, :] == 1) & (local >= 0) & (local < owner_portion)
    order = jnp.arange(per_device, dtype=jnp.int32)[None, :]
    first = jnp.min(
        jnp.where(matches, order * owner_portion + local, per_device * owner_portion), axis=1
    )
    granted = first % owner_portion
    chosen_prompt = (matches & (local == granted[:, None])).astype(F32)
    inside = jnp.arange(LEN, dtype=jnp.int32)[None, :] < my_lengths[:, None]
    chosen = jnp.where(inside[None], chosen_prompt[:, :, None], 0.0).reshape(wide_count, row_total)

    if paired:
        core = [(at, at ^ 1) for at in range(4)]
        across = [(at, at ^ 2) for at in range(4)]
        ticket = lax.ppermute(ticket, "narrow", core)
        far_send, far_keep, held_tokens = column_dots(tokens, value_weight, ticket, columns, True)
        far_arrived = lax.ppermute(far_send, "narrow", core)
        code = code_rows(in_vmem(far_keep), in_vmem(far_arrived))
        near_send, near_keep = column_dots(held_tokens, value_weight, far_keep, columns, False)
        resident, mask = reload_tokens(tokens, chosen, near_keep)
        base = base_rows(
            my_lengths,
            near_keep,
            lax.ppermute(near_send, "narrow", core),
            lax.ppermute(code, "narrow", across),
        )
    else:
        partial_value = jnp.dot(tokens, value_weight, preferred_element_type=F32)
        base = lax.psum_scatter(partial_value, "narrow", scatter_dimension=1, tiled=True)
        base = jnp.where(inside.reshape(row_total, 1), base, 0.0)
        resident, mask = reload_tokens(tokens, chosen, ticket)
    rows = adapter_down_factors.shape[2]
    messages = held[0]
    if not paired:
        part = lax.psum(shrink(resident, chosen, messages, rows, 0, row_total)[0], "narrow")
        return finish(base, mask, part, [], messages, features, 0)
    half = row_total // 2
    send, stacked = shrink(resident, chosen, messages, rows, 2, half)
    (keep,) = shrink(resident, chosen, [stacked], rows, 1, half)
    total, code = code_shrunk(keep, lax.ppermute(send, "narrow", core))
    own = sum_shrunk(total, lax.ppermute(code, "narrow", across), base)
    other = lax.ppermute(own, "narrow", core)
    values = finish(base, mask, own, [], messages, features, 1)
    return finish(base, mask, other, [values], messages, features, 2)


def solution(mesh):
    placed = (
        P(("groups", "wide"), "narrow"),
        P("narrow", None),
        P(("groups", "wide"), "narrow", None),
        P(("groups", "wide"), None, "narrow"),
        P("groups"),
        P("groups"),
        P("groups"),
    )
    return jax.shard_map(
        on_device,
        mesh=mesh,
        in_specs=placed,
        out_specs=P(("groups", "wide"), "narrow"),
        check_vma=False,
    )
```

```python
import functools
import math

import jax
import jax.numpy as jnp
from jax import lax
from jax.experimental import pallas as pl
from jax.experimental.pallas import tpu as pltpu
from jax.sharding import PartitionSpec as P

LEN = 32
CHUNKS = 1
LIMIT = 24 * 2**20
VMEM = pltpu.VMEM
F32 = jnp.float32
BF16 = jnp.bfloat16
STEPS = 32767.0
GRADES = 128.0
SMALL = pl.CostEstimate(flops=1, bytes_accessed=1, transcendentals=0)
LARGE = pl.CostEstimate(flops=10**10, bytes_accessed=1, transcendentals=0)


def whole_block(array_memory=VMEM):
    return pl.BlockSpec(memory_space=array_memory)


def in_vmem(array):
    return pltpu.with_memory_space_constraint(array, VMEM)


def in_hbm(array):
    return pltpu.with_memory_space_constraint(array, pltpu.HBM)


def quarter_copies(weight_hbm, weight_ref, weight_sem, quarters):
    columns = weight_ref.shape[2]
    return [
        pltpu.make_async_copy(
            weight_hbm.at[:, pl.ds(pl.multiple_of(quarter * columns, columns), columns)],
            weight_ref.at[at],
            weight_sem.at[at],
        )
        for at, quarter in enumerate(quarters)
    ]


def pack_kernel(wide_count, per_device, *refs):
    message_count = wide_count * CHUNKS
    loads_in, refs = refs[:5], refs[5:]
    messages, refs = refs[:message_count], refs[message_count:]
    ticket_ref, settings_ref, *refs = refs
    ticket_ref[...] = jnp.zeros_like(ticket_ref)
    choice_ref, mask_ref, down_ref, up_ref, length_ref, load_sem = refs
    owner_portion, rank, features = down_ref.shape
    columns = up_ref.shape[2]
    rows = rank // CHUNKS
    loads = [
        pltpu.make_async_copy(source, target, load_sem.at[at])
        for at, (source, target) in enumerate(zip(loads_in, refs[:5]))
    ]
    for copy in loads:
        copy.start()
    loads[0].wait()
    loads[1].wait()
    me = lax.axis_index("wide")
    choice = choice_ref[...]
    prompt = lax.broadcasted_iota(jnp.int32, choice.shape, 1)
    local = choice - me * owner_portion
    wanted = (mask_ref[...] == 1) & (local >= 0) & (local < owner_portion)
    top = jnp.float32(2.0**24)
    key = jnp.where(wanted, (prompt * owner_portion + local).astype(F32), top)
    adapters = []
    many = (wide_count, choice.shape[1])
    reader = lax.rem(me + lax.broadcasted_iota(jnp.int32, many, 0), wide_count)
    place = lax.broadcasted_iota(jnp.int32, many, 1) - reader * per_device
    inside = (place >= 0) & (place < per_device)
    firsts = jnp.min(jnp.where(inside, key, top), axis=1, keepdims=True)
    found = jnp.where(firsts < top, firsts, 0.0).astype(jnp.int32)
    for shift in range(wide_count):
        adapter = lax.rem(found[shift, 0], owner_portion)
        adapters.append(adapter)
    loads[2].wait()
    loads[3].wait()
    for at, adapter in enumerate(adapters):
        for chunk in range(CHUNKS):
            out = messages[at * CHUNKS + chunk]
            span = pl.ds(chunk * rows, rows)
            out[:, pl.ds(0, features)] = down_ref[adapter, span, :]
            out[:, pl.ds(features, columns)] = up_ref[adapter, span, :]
    loads[4].wait()
    for at, source in enumerate((choice_ref, mask_ref, length_ref)):
        settings_ref[pl.ds(at, 1), :] = source[...]


def pack_messages(choice, mask, lengths, down, up, wide_count, per_device):
    rank, features = down.shape[1:]
    columns = up.shape[2]
    count = wide_count * CHUNKS
    hbm = whole_block(pl.ANY)
    operands = [choice, mask, down, up, lengths]
    scratch = [VMEM(operand.shape, operand.dtype) for operand in operands]
    scratch += [pltpu.SemaphoreType.DMA((5,))]
    out_shape = [VMEM((rank // CHUNKS, features + columns), BF16)] * count
    out_specs = [whole_block()] * (count + 2)
    out_shape += [jax.ShapeDtypeStruct((8, 128), F32), jax.ShapeDtypeStruct((3, choice.shape[1]), jnp.int32)]
    out = pl.pallas_call(
        functools.partial(pack_kernel, wide_count, per_device),
        out_shape=out_shape,
        in_specs=[hbm] * len(operands),
        out_specs=out_specs,
        scratch_shapes=scratch,
        compiler_params=pltpu.CompilerParams(vmem_limit_bytes=LIMIT),
        cost_estimate=SMALL,
        name="pack_messages",
    )(*[in_hbm(operand) for operand in operands])
    return [out[shift * CHUNKS : (shift + 1) * CHUNKS] for shift in range(wide_count)], *out[count:]


def grade_of(size):
    return jnp.ceil(jnp.log(jnp.maximum(size, 2.0**-120)) * (GRADES / math.log(2.0)))


def size_of(grade):
    return jnp.exp2(grade * (1.0 / GRADES)) * (1.0 / STEPS)


def coded(total, grade):
    scaled = total * jnp.exp2(grade * (-1.0 / GRADES)) * STEPS
    return jnp.clip(jnp.round(scaled), -STEPS, STEPS).astype(jnp.int32).astype(jnp.int16)


def code_kernel(keep_ref, arrived_ref, code_ref):
    block = 128
    row_total, columns = keep_ref.shape
    grades = []
    for at in range(row_total // block):
        span = pl.ds(at * block, block)
        total = keep_ref[span, :] + arrived_ref[span, :]
        grade = grade_of(jnp.max(jnp.abs(total), axis=1, keepdims=True))
        code_ref[span, :] = coded(total, grade)
        grades.append(jnp.broadcast_to(grade, (block, block)).T[:1, :])
    grades = jnp.concatenate(grades + [jnp.zeros((16 - len(grades), block), F32)], axis=0)
    grades = jnp.concatenate([grades, jnp.zeros((16, columns - block), F32)], axis=1)
    code_ref[pl.ds(row_total, 16), :] = grades.astype(jnp.int32).astype(jnp.int16)


def code_rows(keep, arrived):
    row_total, columns = keep.shape
    return pl.pallas_call(
        code_kernel,
        out_shape=VMEM((row_total + 16, columns), jnp.int16),
        in_specs=[whole_block()] * 2,
        out_specs=whole_block(),
        compiler_params=pltpu.CompilerParams(vmem_limit_bytes=LIMIT),
        cost_estimate=SMALL,
        name="code_rows",
    )(keep, arrived)


def pair_dots(tokens_ref, weight_ref, weight_copies, send_ref, keep_ref, send_hbm, send_sem):
    block = 256
    spans = [pl.ds(low, block) for low in range(0, tokens_ref.shape[0], block)]
    for span in spans:
        send_ref[span, :] = jnp.dot(tokens_ref[span, :], weight_ref[0], preferred_element_type=F32)
    copy = pltpu.make_async_copy(send_ref, send_hbm, send_sem)
    copy.start()
    weight_copies[1].wait()
    for span in spans:
        keep_ref[span, :] = jnp.dot(tokens_ref[span, :], weight_ref[1], preferred_element_type=F32)
    copy.wait()


def far_kernel(tokens_hbm, weight_hbm, ticket_ref, send_hbm, keep_ref, tokens_ref, *scratch):
    weight_ref, send_ref, weight_sem, send_sem, token_sem = scratch
    narrow_at = lax.axis_index("narrow")
    mine = lax.rem(narrow_at, 2)
    chip = 2 * ((narrow_at // 2) ^ 1)
    weight_copies = quarter_copies(weight_hbm, weight_ref, weight_sem, (chip + 1 - mine, chip + mine))
    token_copy = pltpu.make_async_copy(tokens_hbm, tokens_ref, token_sem)
    weight_copies[0].start()
    token_copy.start()
    weight_copies[1].start()
    weight_copies[0].wait()
    token_copy.wait()
    pair_dots(tokens_ref, weight_ref, weight_copies, send_ref, keep_ref, send_hbm, send_sem)


def near_kernel(tokens_ref, weight_hbm, ticket_ref, send_hbm, keep_ref, *scratch):
    weight_ref, send_ref, weight_sem, send_sem = scratch
    narrow_at = lax.axis_index("narrow")
    mine = lax.rem(narrow_at, 2)
    chip = 2 * (narrow_at // 2)
    weight_copies = quarter_copies(weight_hbm, weight_ref, weight_sem, (chip + 1 - mine, chip + mine))
    for copy in weight_copies:
        copy.start()
    weight_copies[0].wait()
    pair_dots(tokens_ref, weight_ref, weight_copies, send_ref, keep_ref, send_hbm, send_sem)


def column_dots(tokens, weight, ticket, columns, far):
    row_total, features = tokens.shape
    hbm = whole_block(pl.ANY)
    out_shape = [pltpu.HBM((row_total, columns), F32), VMEM((row_total, columns), F32)]
    scratch = [
        VMEM((2, features, columns), BF16),
        VMEM((row_total, columns), F32),
        pltpu.SemaphoreType.DMA((2,)),
        pltpu.SemaphoreType.DMA,
    ]
    if far:
        out_shape.append(VMEM(tokens.shape, BF16))
        scratch.append(pltpu.SemaphoreType.DMA)
    return pl.pallas_call(
        far_kernel if far else near_kernel,
        out_shape=out_shape,
        in_specs=[hbm if far else whole_block(), hbm, hbm],
        out_specs=[hbm] + [whole_block()] * (len(out_shape) - 1),
        scratch_shapes=scratch,
        compiler_params=pltpu.CompilerParams(vmem_limit_bytes=LIMIT),
        cost_estimate=SMALL if far else LARGE,
        name="far_columns" if far else "near_columns",
    )(in_hbm(tokens) if far else tokens, in_hbm(weight), ticket)


def reload_kernel(tokens_hbm, chosen_ref, ticket_ref, tokens_ref, mask_ref, token_sem):
    copy = pltpu.make_async_copy(tokens_hbm, tokens_ref, token_sem)
    copy.start()
    lanes = 128
    for low in range(0, tokens_ref.shape[0], lanes):
        for at in range(chosen_ref.shape[0]):
            row = chosen_ref[pl.ds(at, 1), pl.ds(low, lanes)]
            column = jnp.broadcast_to(row, (lanes, lanes)).T
            mask_ref[pl.ds(low, lanes), pl.ds(at * lanes, lanes)] = column.astype(BF16)
    copy.wait()


def reload_tokens(tokens, chosen, ticket):
    hbm = whole_block(pl.ANY)
    return pl.pallas_call(
        reload_kernel,
        out_shape=[VMEM(tokens.shape, BF16), VMEM((tokens.shape[0], chosen.shape[0] * 128), BF16)],
        in_specs=[hbm, whole_block(), hbm],
        out_specs=[whole_block()] * 2,
        scratch_shapes=[pltpu.SemaphoreType.DMA],
        compiler_params=pltpu.CompilerParams(vmem_limit_bytes=LIMIT),
        cost_estimate=SMALL,
        name="reload_tokens",
    )(in_hbm(tokens), chosen, ticket)


def base_kernel(length_ref, keep_ref, arrived_ref, code_ref, out_ref):
    row_total, columns = out_ref.shape
    block = 128
    position = lax.broadcasted_iota(jnp.int32, (LEN, columns), 0)
    grades = code_ref[pl.ds(row_total, 16), :].astype(jnp.int32).astype(F32)
    sizes = size_of(grades[:, :block])
    for at in range(row_total // block):
        span = pl.ds(at * block, block)
        size = jnp.broadcast_to(sizes[at : at + 1, :], (block, block)).T
        size = jnp.concatenate([size] * (columns // block), axis=1)
        crossed = code_ref[span, :].astype(jnp.int32).astype(F32) * size
        total = keep_ref[span, :] + arrived_ref[span, :] + crossed
        for prompt in range(block // LEN):
            low = at * block + prompt * LEN
            live = position < length_ref[low // LEN]
            piece = total[prompt * LEN : (prompt + 1) * LEN, :]
            out_ref[pl.ds(low, LEN), :] = jnp.where(live, piece, 0.0)


def base_rows(lengths, keep, arrived, code):
    return pl.pallas_call(
        base_kernel,
        out_shape=VMEM(keep.shape, F32),
        in_specs=[whole_block(pltpu.SMEM)] + [whole_block()] * 3,
        out_specs=whole_block(),
        compiler_params=pltpu.CompilerParams(vmem_limit_bytes=LIMIT),
        cost_estimate=SMALL,
        name="base_rows",
    )(lengths, keep, arrived, code)


def piece_start(kind, length):
    if kind == 0:
        return 0
    mine = lax.rem(lax.axis_index("narrow"), 2)
    return pl.multiple_of((mine if kind == 1 else 1 - mine) * length, length)


def shrink_kernel(kind, stacking, tokens_ref, chosen_ref, *refs):
    if stacking:
        messages, (out_ref, stacked) = refs[:-2], refs[-2:]
    else:
        stacked, out_ref = refs
    rows, row_total = out_ref.shape
    features = tokens_ref.shape[1]
    count = stacked.shape[0] // rows
    block = 256
    start = piece_start(kind, row_total)
    if stacking:
        for at, message in enumerate(messages):
            stacked[pl.ds(at * rows, rows), :] = message[:, :features]
    for low in range(0, row_total, block):
        span = pl.ds(pl.multiple_of(start + low, block), block)
        sums = lax.dot_general(
            tokens_ref[span, :], stacked[...], (((1,), (1,)), ((), ())), preferred_element_type=F32
        ).T
        asked = chosen_ref[:, span] > 0
        total = None
        for at in range(count):
            term = jnp.where(asked[at : at + 1, :], sums[at * rows : (at + 1) * rows, :], 0.0)
            total = term if total is None else total + term
        out_ref[:, pl.ds(low, block)] = total


def shrink(tokens, chosen, factors, rows, kind, row_total):
    features = tokens.shape[1]
    stacking = len(factors) > 1
    out_shape = [jax.ShapeDtypeStruct((rows, row_total), F32)]
    if stacking:
        out_shape.append(VMEM((len(factors) * rows, features), BF16))
    return pl.pallas_call(
        functools.partial(shrink_kernel, kind, stacking),
        out_shape=out_shape,
        in_specs=[whole_block()] * (2 + len(factors)),
        out_specs=[whole_block()] * len(out_shape),
        compiler_params=pltpu.CompilerParams(vmem_limit_bytes=LIMIT),
        cost_estimate=SMALL,
        name="shrink",
    )(tokens, chosen, *factors)


def shrunk_code_kernel(keep_ref, arrived_ref, total_ref, code_ref):
    rows, row_total = keep_ref.shape
    total = keep_ref[...] + arrived_ref[...]
    total_ref[...] = total
    grade = grade_of(jnp.max(jnp.abs(total), axis=0, keepdims=True))
    code_ref[pl.ds(0, rows), :] = coded(total, grade)
    grades = jnp.concatenate([grade, jnp.zeros((15, row_total), F32)], axis=0)
    code_ref[pl.ds(rows, 16), :] = grades.astype(jnp.int32).astype(jnp.int16)


def code_shrunk(keep, arrived):
    rows, row_total = keep.shape
    return pl.pallas_call(
        shrunk_code_kernel,
        out_shape=[
            jax.ShapeDtypeStruct((rows, row_total), F32),
            jax.ShapeDtypeStruct((rows + 16, row_total), jnp.int16),
        ],
        in_specs=[whole_block()] * 2,
        out_specs=[whole_block()] * 2,
        compiler_params=pltpu.CompilerParams(vmem_limit_bytes=LIMIT),
        cost_estimate=SMALL,
        name="code_shrunk",
    )(keep, arrived)


def sum_kernel(total_ref, code_ref, ticket_ref, out_ref):
    rows = total_ref.shape[0]
    size = size_of(code_ref[pl.ds(rows, 16), :].astype(jnp.int32).astype(F32)[:1, :])
    out_ref[...] = total_ref[...] + code_ref[pl.ds(0, rows), :].astype(jnp.int32).astype(F32) * size


def sum_shrunk(total, code, ticket):
    return pl.pallas_call(
        sum_kernel,
        out_shape=jax.ShapeDtypeStruct(total.shape, F32),
        in_specs=[whole_block()] * 2 + [whole_block(pl.ANY)],
        out_specs=whole_block(),
        compiler_params=pltpu.CompilerParams(vmem_limit_bytes=LIMIT),
        cost_estimate=SMALL,
        name="sum_shrunk",
    )(total, code, ticket)


def finish_kernel(kind, features, base_ref, mask_ref, part_ref, *refs):
    if kind == 2:
        refs = refs[1:]
    messages, (out_hbm, out_ref, stacked, sem) = refs[:-4], refs[-4:]
    rows = part_ref.shape[0]
    for at, message in enumerate(messages):
        factor = message[:, features:]
        stacked[pl.ds(2 * at * rows, rows), :] = factor
        stacked[pl.ds((2 * at + 1) * rows, rows), :] = factor
    row_total, columns = out_ref.shape
    block = 256
    start = piece_start(kind, row_total)
    copies = []
    for low in range(0, row_total, block):
        here = pl.ds(low, block)
        span = pl.ds(pl.multiple_of(start + low, block), block)
        shrunk = part_ref[:, here]
        high = shrunk.astype(BF16).astype(F32)
        both = jnp.concatenate([high, shrunk - high], axis=0).T.astype(BF16)
        spread = jnp.concatenate([both] * len(messages), axis=1) * mask_ref[span, :]
        total = base_ref[span, :] + jnp.dot(spread, stacked[...], preferred_element_type=F32)
        out_ref[here, :] = total.astype(BF16)
        copies.append(pltpu.make_async_copy(out_ref.at[here, :], out_hbm.at[span, :], sem.at[low // block]))
        copies[-1].start()
    for copy in copies:
        copy.wait()


def finish(base, mask, part, earlier, messages, features, kind):
    columns = base.shape[1]
    count = len(messages)
    rows, row_total = part.shape
    operands = [base, mask, part, *earlier, *messages]
    hbm = whole_block(pl.ANY)
    in_specs = [whole_block()] * 3
    aliases = {len(in_specs): 0} if earlier else {}
    in_specs += [hbm] * len(earlier) + [whole_block()] * count
    return pl.pallas_call(
        functools.partial(finish_kernel, kind, features),
        out_shape=jax.ShapeDtypeStruct(base.shape, BF16),
        in_specs=in_specs,
        out_specs=hbm,
        input_output_aliases=aliases,
        scratch_shapes=[
            VMEM((row_total, columns), BF16),
            VMEM((2 * count * rows, columns), BF16),
            pltpu.SemaphoreType.DMA((row_total // 256,)),
        ],
        compiler_params=pltpu.CompilerParams(vmem_limit_bytes=LIMIT),
        cost_estimate=SMALL,
        name="finish",
    )(*operands)


def on_device(
    tokens,
    value_weight,
    adapter_down_factors,
    adapter_up_factors,
    adapter_choice_index,
    adapter_mask,
    prompt_token_length,
):
    wide_count = lax.axis_size("wide")
    narrow_count = lax.axis_size("narrow")
    wide_at = lax.axis_index("wide")
    owner_portion = adapter_down_factors.shape[0]
    row_total, features = tokens.shape
    per_device = row_total // LEN
    columns = adapter_up_factors.shape[2]

    paired = narrow_count == 4
    sent, ticket, settings = pack_messages(
        adapter_choice_index.reshape(1, -1),
        adapter_mask.reshape(1, -1),
        prompt_token_length.reshape(1, -1),
        jnp.swapaxes(adapter_down_factors, 1, 2),
        adapter_up_factors,
        wide_count,
        per_device,
    )
    held = [[sent[0][chunk]] for chunk in range(CHUNKS)]
    for chunk in range(CHUNKS):
        for shift in range(1, wide_count):
            ring = [(at, (at + shift) % wide_count) for at in range(wide_count)]
            held[chunk].append(lax.ppermute(sent[shift][chunk], "wide", ring))

    my_settings = lax.dynamic_slice_in_dim(settings, wide_at * per_device, per_device, axis=1)
    my_choice, my_mask, my_lengths = my_settings[0], my_settings[1], my_settings[2]
    owners = (wide_at - jnp.arange(wide_count, dtype=jnp.int32) + wide_count) % wide_count
    local = my_choice[None, :] - owners[:, None] * owner_portion
    matches = (my_mask[None, :] == 1) & (local >= 0) & (local < owner_portion)
    order = jnp.arange(per_device, dtype=jnp.int32)[None, :]
    first = jnp.min(
        jnp.where(matches, order * owner_portion + local, per_device * owner_portion), axis=1
    )
    granted = first % owner_portion
    chosen_prompt = (matches & (local == granted[:, None])).astype(F32)
    inside = jnp.arange(LEN, dtype=jnp.int32)[None, :] < my_lengths[:, None]
    chosen = jnp.where(inside[None], chosen_prompt[:, :, None], 0.0).reshape(wide_count, row_total)

    if paired:
        core = [(at, at ^ 1) for at in range(4)]
        across = [(at, at ^ 2) for at in range(4)]
        ticket = lax.ppermute(ticket, "narrow", core)
        far_send, far_keep, held_tokens = column_dots(tokens, value_weight, ticket, columns, True)
        far_arrived = lax.ppermute(far_send, "narrow", core)
        code = code_rows(in_vmem(far_keep), in_vmem(far_arrived))
        near_send, near_keep = column_dots(held_tokens, value_weight, far_keep, columns, False)
        resident, mask = reload_tokens(tokens, chosen, near_keep)
        base = base_rows(
            my_lengths,
            near_keep,
            lax.ppermute(near_send, "narrow", core),
            lax.ppermute(code, "narrow", across),
        )
    else:
        partial_value = jnp.dot(tokens, value_weight, preferred_element_type=F32)
        base = lax.psum_scatter(partial_value, "narrow", scatter_dimension=1, tiled=True)
        base = jnp.where(inside.reshape(row_total, 1), base, 0.0)
        resident, mask = reload_tokens(tokens, chosen, ticket)
    rows = adapter_down_factors.shape[2]
    messages = held[0]
    if not paired:
        part = lax.psum(shrink(resident, chosen, messages, rows, 0, row_total)[0], "narrow")
        return finish(base, mask, part, [], messages, features, 0)
    half = row_total // 2
    send, stacked = shrink(resident, chosen, messages, rows, 2, half)
    (keep,) = shrink(resident, chosen, [stacked], rows, 1, half)
    total, code = code_shrunk(keep, lax.ppermute(send, "narrow", core))
    own = sum_shrunk(total, lax.ppermute(code, "narrow", across), base)
    other = lax.ppermute(own, "narrow", core)
    values = finish(base, mask, own, [], messages, features, 1)
    return finish(base, mask, other, [values], messages, features, 2)


def solution(mesh):
    placed = (
        P(("groups", "wide"), "narrow"),
        P("narrow", None),
        P(("groups", "wide"), "narrow", None),
        P(("groups", "wide"), None, "narrow"),
        P("groups"),
        P("groups"),
        P("groups"),
    )
    return jax.shard_map(
        on_device,
        mesh=mesh,
        in_specs=placed,
        out_specs=P(("groups", "wide"), "narrow"),
        check_vma=False,
    )
```
